512 devices in a mesh: dp: 4 (over y), seq: 16 (over x, z_hi, core), head: 8 (over z_lo).
Axes of the slice: x: 4, y: 4, z: 16 (z_hi: 2, z_lo: 8; z = z_hi * 8 + z_lo), core: 2. Of those that a mesh axis runs over, the one named last changes fastest.
Arguments:
- projected: bfloat16 [4, 4096, 4, 1024], P('dp', ('seq', 'head')), may hold values from -6 to 6
- cotangent: bfloat16 [4, 4096, 1024], P('dp', ('seq', 'head')), may hold values from -6 to 6
- out_weight: bfloat16 [1024, 1024], P('head'), may hold values from -0.1875 to 0.1875
- time_bias: float32 [8, 16], P('head'), may hold values from -1.5 to 1.5
- block_lists: int32 [4, 32, 24], P('dp'), may hold values from -1 to 31, as said below
- stamps: int32 [4, 4096], P('dp'), may hold values from 0 to 6144, as said below
Outputs:
- layer_out: bfloat16 [4, 4096, 1024], P('dp', ('seq', 'head'))
- input_grads: bfloat16 [4, 4096, 4, 1024], P('dp', ('seq', 'head'))
- weight_grad: float32 [1024, 1024], P('head')
- bias_grad: float32 [8, 16], P('head')
The draws below stay inside these ranges and needn't reach their ends.
Inputs may be any that keep to these rules, and one draw needn't show every extreme that they name: `block_lists`: entry 0 of row r is r itself; the next n - 1 entries are distinct blocks below r; the remaining entries are -1; n runs from 1 to 24, and in every history some row has all 24 entries. `stamps`: never falls along a history and rises by at most 3 from one action to the next; the first action of each history has stamp 0 and the last one the largest stamp.
All inputs are finite; a program needn't handle non-finite values.
Results may differ from the reference program's by a relative error of at most 0.0057.
Values may be sent and summed in bfloat16 or wider, within the bound.
No kernel may reach another device: no remote copies, remote signals or barrier semaphores. Data moves between devices by JAX's collectives and lax.ppermute only.
A program may use at most 64 MiB of HBM per device.

```python
import jax
import jax.numpy as jnp
from jax import lax

HEADS = 8
HEAD_DIM = 128
D = 1024
BLOCK = 128
BUCKETS = 16
BLOCKS = 32
HIST_LEN = 4096
LIST_MAX = 24
GROUPS = 4


def draw_block_lists(key, part):
    key = jax.random.fold_in(key, 11)
    noise_key = jax.random.fold_in(key, 1)
    heavy_key = jax.random.fold_in(key, 2)
    light_key = jax.random.fold_in(key, 3)
    blocks_idx = jnp.arange(BLOCKS, dtype=jnp.int32)
    noise = jax.random.randint(noise_key, (GROUPS, BLOCKS, BLOCKS), 0, 1 << 20)
    ranking = noise * BLOCKS + blocks_idx[None, None, :]
    ranking = jnp.where(blocks_idx[None, None, :] < blocks_idx[None, :, None], ranking, (1 << 30) + blocks_idx[None, None, :])
    earlier = jnp.argsort(ranking, axis=-1, stable=True)[..., :LIST_MAX - 1].astype(jnp.int32)
    heavy = jax.random.randint(heavy_key, (GROUPS, BLOCKS), 0, 4) == 0
    light = jax.random.randint(light_key, (GROUPS, BLOCKS), 1, LIST_MAX // 2 + 1)
    wanted = jnp.where(heavy, LIST_MAX, light)
    wanted = jnp.minimum(wanted, blocks_idx[None, :] + 1)
    wanted = wanted.at[:, BLOCKS - 1].set(LIST_MAX)
    positions = jnp.arange(LIST_MAX - 1, dtype=jnp.int32)
    earlier = jnp.where(positions[None, None, :] < (wanted - 1)[..., None], earlier, -1)
    own_block = jnp.broadcast_to(blocks_idx[None, :, None], (GROUPS, BLOCKS, 1))
    return jnp.concatenate([own_block, earlier], -1).astype(jnp.int32)


def draw_stamps(key, part):
    key = jax.random.fold_in(key, 23)
    steps_up = jax.random.randint(key, (GROUPS, HIST_LEN), 0, 4)
    steps_up = steps_up.at[:, HIST_LEN - 1].set(3)
    places = jnp.arange(HIST_LEN, dtype=jnp.int32)
    odd = (places % 2 == 1)[None, :]
    return (3 * (places // 2)[None, :] + jnp.where(odd, steps_up, 0)).astype(jnp.int32)


def block_levels(rng, shape, cuts, low, top_value):
    gain, own = 1.0, jax.random.fold_in(rng, 6)
    for axis_at, parts in cuts:
        steps = jnp.exp(jax.random.uniform(jax.random.fold_in(own, axis_at), (parts,), jnp.float32, low / len(cuts), top_value / len(cuts)))
        gain = gain * jnp.repeat(steps, shape[axis_at] // parts).reshape([-1 if axis == axis_at else 1 for axis in range(len(shape))])
    return gain


def scatter_about(own_key, shape, width, limit, shards=(), held_as=jnp.bfloat16):
    values = width * jax.random.normal(own_key, shape, jnp.float32)
    if shards:
        values = values * block_levels(own_key, shape, shards, -0.22, 0.18)
    return jnp.clip(values, -limit, limit).astype(held_as)


def setup_inputs(seed: int = 0) -> dict:
    key_of = jax.random.split(jax.random.key(seed), 7)
    projected = scatter_about(key_of[0], (GROUPS, HIST_LEN, 4, D), 1.0, 6.0, ((0, 4), (1, 128)))
    cotangent = scatter_about(key_of[1], (GROUPS, HIST_LEN, D), 1.0, 6.0, ((0, 4), (1, 128)))
    out_weight = scatter_about(key_of[2], (D, D), D ** -0.5, 0.1875, ((0, 8),))
    time_bias = jnp.clip(jax.random.uniform(key_of[3], (HEADS, BUCKETS), jnp.float32, -1.5, 1.5) * block_levels(key_of[3], (HEADS, BUCKETS), ((0, 8),), -0.4, 0.0), -1.5, 1.5)
    block_lists = draw_block_lists(jax.random.fold_in(key_of[6], 71), 0)
    stamps = draw_stamps(jax.random.fold_in(key_of[6], 71), 0)
    return dict(projected=projected, cotangent=cotangent, out_weight=out_weight, time_bias=time_bias, block_lists=block_lists, stamps=stamps)


eps = 1e-05

def rounded(values):
    return lax.optimization_barrier(values.astype(jnp.bfloat16)).astype(jnp.float32)

def bucketize(spread):
    spread = jnp.maximum(spread, 0)
    powers = 2 ** jnp.arange(BUCKETS - 1, dtype=jnp.int32)
    return lax.optimization_barrier(jnp.sum((spread[..., None] >= powers).astype(jnp.int32), axis=-1))

def one_history(projected, cotangent, lists, stamps_row, out_weight, time_bias):
    length = projected.shape[0]
    nblocks = length // BLOCK
    score_scale = HEAD_DIM ** (-0.5)
    arranged = projected.reshape(length, 4, HEADS, HEAD_DIM)
    query_blocks = arranged[:, 0].reshape(nblocks, BLOCK, HEADS, HEAD_DIM)
    key_blocks = arranged[:, 1].reshape(nblocks, BLOCK, HEADS, HEAD_DIM)
    value_blocks = arranged[:, 2].reshape(nblocks, BLOCK, HEADS, HEAD_DIM)
    gate_flat = arranged[:, 3].reshape(length, D)
    within = jnp.arange(BLOCK, dtype=jnp.int32)

    def tile(block):
        entries = lists[block]
        chosen = jnp.maximum(entries, 0).astype(jnp.int32)
        key_sel = key_blocks[chosen].astype(jnp.float32)
        scores = jnp.einsum('qhd,mkhd->hqmk', query_blocks[block].astype(jnp.float32), key_sel) * score_scale
        query_pos = block * BLOCK + within
        key_pos = chosen[:, None] * BLOCK + within[None, :]
        spread = stamps_row[query_pos][:, None, None] - stamps_row[key_pos][None]
        buckets = bucketize(spread)
        scores = scores + time_bias[:, buckets]
        allowed = (entries >= 0)[None, :, None] & (key_pos[None] <= query_pos[:, None, None])
        listed = jnp.sum((entries >= 0).astype(jnp.int32))
        counts = (BLOCK * (listed - 1) + within + 1).astype(jnp.float32)
        return (scores, allowed, buckets, chosen, counts)

    def forward_block(block):
        scores, allowed, buckets, chosen, counts = tile(block)
        weights = rounded(jnp.where(allowed[None], jax.nn.silu(scores), 0.0) / counts[None, :, None, None])
        return jnp.einsum('hqmk,mkhd->qhd', weights, value_blocks[chosen].astype(jnp.float32))
    attended = lax.map(forward_block, jnp.arange(nblocks, dtype=jnp.int32))
    flat = attended.reshape(length, D)
    row_mean = lax.optimization_barrier(jnp.mean(flat, -1, keepdims=True))
    power = lax.optimization_barrier(jnp.mean(flat * flat, -1, keepdims=True))
    inverse = lax.rsqrt(power - row_mean * row_mean + eps)
    normed = (flat - row_mean) * inverse
    gated = (normed * gate_flat.astype(jnp.float32)).astype(jnp.bfloat16)
    layer_out = jnp.dot(gated, out_weight, preferred_element_type=jnp.float32).astype(jnp.bfloat16)
    gated_grad = jnp.dot(cotangent, out_weight.T, preferred_element_type=jnp.float32)
    weight_grad = jnp.dot(gated.T, cotangent, preferred_element_type=jnp.float32)
    grad_u = (gated_grad * normed).astype(jnp.bfloat16)
    normed_grad = gated_grad * gate_flat.astype(jnp.float32)
    first_mean = lax.optimization_barrier(jnp.mean(normed_grad, -1, keepdims=True))
    second_mean = lax.optimization_barrier(jnp.mean(normed_grad * normed, -1, keepdims=True))
    attended_grad = ((normed_grad - first_mean - normed * second_mean) * inverse).astype(jnp.bfloat16)
    grad_blocks = attended_grad.reshape(nblocks, BLOCK, HEADS, HEAD_DIM)

    def backward_block(carry, block):
        key_acc, value_acc, bias_acc = carry
        scores, allowed, buckets, chosen, counts = tile(block)
        weights = rounded(jnp.where(allowed[None], jax.nn.silu(scores), 0.0) / counts[None, :, None, None])
        grad_tile = grad_blocks[block].astype(jnp.float32)
        prob_grad = jnp.einsum('qhd,mkhd->hqmk', grad_tile, value_blocks[chosen].astype(jnp.float32))
        sigmoid = jax.nn.sigmoid(scores)
        score_grad = jnp.where(allowed[None], prob_grad * sigmoid * (1.0 + scores * (1.0 - sigmoid)), 0.0) / counts[None, :, None, None]
        flat_grad = jnp.moveaxis(score_grad, 0, -1).reshape(-1, HEADS)
        bias_acc = bias_acc + jax.ops.segment_sum(flat_grad, buckets.reshape(-1), BUCKETS).T
        score_low = rounded(score_grad)
        query_grad = jnp.einsum('hqmk,mkhd->qhd', score_low, key_blocks[chosen].astype(jnp.float32)) * score_scale
        key_acc = key_acc.at[chosen].add(jnp.einsum('hqmk,qhd->mkhd', score_low, query_blocks[block].astype(jnp.float32)))
        value_acc = value_acc.at[chosen].add(jnp.einsum('hqmk,qhd->mkhd', weights, grad_tile))
        return ((key_acc, value_acc, bias_acc), query_grad.astype(jnp.bfloat16))
    empty = jnp.zeros((nblocks, BLOCK, HEADS, HEAD_DIM), jnp.float32)
    start = (empty, empty, jnp.zeros((HEADS, BUCKETS), jnp.float32))
    (key_acc, value_acc, bias_acc), query_grads = lax.scan(backward_block, start, jnp.arange(nblocks, dtype=jnp.int32))
    grad_q = query_grads.reshape(length, D)
    grad_k = (key_acc * score_scale).astype(jnp.bfloat16).reshape(length, D)
    grad_v = value_acc.astype(jnp.bfloat16).reshape(length, D)
    input_grads = jnp.stack([grad_q, grad_k, grad_v, grad_u], 1)
    return (layer_out, input_grads, weight_grad, bias_acc)

def reference(projected, cotangent, out_weight, time_bias, block_lists, stamps):

    def one(inputs):
        return one_history(inputs[0], inputs[1], inputs[2], inputs[3], out_weight, time_bias)
    layer_out, input_grads, weight_parts, bias_parts = lax.map(one, (projected, cotangent, block_lists, stamps))
    return (layer_out, input_grads, lax.optimization_barrier(jnp.sum(weight_parts, 0)), lax.optimization_barrier(jnp.sum(bias_parts, 0)))
```

```python
import functools

import jax
import jax.numpy as jnp
from jax import lax
from jax.experimental import pallas as pl
from jax.experimental.pallas import tpu as pltpu
from jax.sharding import Mesh, PartitionSpec as P

HEADS = 8
HEAD_DIM = 128
D = 1024
BLOCK = 128
BUCKETS = 16
BLOCKS = 32
LIST_MAX = 24
EPS = 1e-05
SCALE = HEAD_DIM ** (-0.5)

SEQ = ("x", "zh", "core")
ZLINE = ("zh", "head")
TEAM = ("dp", "x", "zh", "core")
VMEM_LIMIT = 48 * 1024 * 1024
f32 = jnp.float32
bf16 = jnp.bfloat16

FWD_GROUP = 4
BWD_GROUP = 2


def nt_dot(a, b):
    return lax.dot_general(a, b, (((1,), (1,)), ((), ())), preferred_element_type=f32)


def nn_dot(a, b):
    return lax.dot_general(a, b, (((1,), (0,)), ((), ())), preferred_element_type=f32)


def half_bias(spread, bias_ref):
    bias = jnp.full((BLOCK, BLOCK), bias_ref[0] * 0.5, f32)
    for e in range(BUCKETS - 1):
        bias = jnp.where(spread >= float(2**e), bias_ref[e + 1] * 0.5, bias)
    return bias


def column_of(row):
    return jnp.transpose(jnp.broadcast_to(row, (BLOCK, BLOCK)))


def slot_setup(slot, blk_ref, n_ref, stamps_ref):
    listed = n_ref[slot]
    block = blk_ref[slot, 0]
    query_stamps = column_of(stamps_ref[pl.ds(block, 1), :].astype(f32))
    within = lax.broadcasted_iota(jnp.int32, (BLOCK, BLOCK), 0)
    counts = (BLOCK * (listed - 1) + within + 1).astype(f32)
    return listed, query_stamps, 1.0 / counts


def causal():
    rows = lax.broadcasted_iota(jnp.int32, (BLOCK, BLOCK), 0)
    cols = lax.broadcasted_iota(jnp.int32, (BLOCK, BLOCK), 1)
    return cols <= rows


def load_pairs(own_ref, other_ref, kv, sems):
    rows = own_ref.shape[0]
    first = pltpu.make_async_copy(own_ref, kv.at[pl.ds(0, rows)], sems.at[0])
    second = pltpu.make_async_copy(other_ref, kv.at[pl.ds(rows, rows)], sems.at[1])
    first.start()
    second.start()
    first.wait()
    second.wait()


def attend_kernel(
    pos_ref, blk_ref, n_ref, bias_ref, stamps_ref, q_ref, own_ref, other_ref, out_ref, kv, sems
):
    load_pairs(own_ref, other_ref, kv, sems)
    for slot in range(2):
        listed, query_stamps, inverse = slot_setup(slot, blk_ref, n_ref, stamps_ref)
        query = q_ref[slot * BLOCK : (slot + 1) * BLOCK, :]

        def tile(entry, share):
            rows = pl.ds(pl.multiple_of(pos_ref[slot, entry] * BLOCK, BLOCK), BLOCK)
            key = kv[rows, 0:HEAD_DIM]
            value = kv[rows, HEAD_DIM : 2 * HEAD_DIM]
            spread = query_stamps - stamps_ref[pl.ds(blk_ref[slot, entry], 1), :].astype(f32)
            half = nt_dot(query, key) * (0.5 * SCALE) + half_bias(spread, bias_ref)
            weights = ((half + half * jnp.tanh(half)) * share).astype(bf16)
            return nn_dot(weights, value)

        total = tile(0, jnp.where(causal(), inverse, 0.0))

        def group(step, acc):
            for j in range(FWD_GROUP):
                entry = 1 + step * FWD_GROUP + j
                valid = (entry < listed).astype(f32)
                acc = acc + tile(jnp.minimum(entry, LIST_MAX - 1), inverse * valid)
            return acc

        steps = (listed - 1 + FWD_GROUP - 1) // FWD_GROUP
        out_ref[slot * BLOCK : (slot + 1) * BLOCK, :] = lax.fori_loop(0, steps, group, total)


def grads_kernel(
    pos_ref,
    blk_ref,
    n_ref,
    bias_ref,
    stamps_ref,
    q_ref,
    g_ref,
    own_ref,
    other_ref,
    dq_ref,
    own_acc_ref,
    other_acc_ref,
    bias_acc_ref,
    kv,
    acc,
    sems,
):
    rows_half = BLOCKS // 2
    acc[...] = jnp.zeros(acc.shape, f32)
    bias_acc_ref[...] = jnp.zeros(bias_acc_ref.shape, f32)
    load_pairs(own_ref, other_ref, kv, sems)
    for slot in range(2):
        listed, query_stamps, inverse = slot_setup(slot, blk_ref, n_ref, stamps_ref)
        query = q_ref[slot * BLOCK : (slot + 1) * BLOCK, :]
        grad = g_ref[slot * BLOCK : (slot + 1) * BLOCK, :]
        query_t = jnp.transpose(query.astype(f32)).astype(bf16)
        grad_t = jnp.transpose(grad.astype(f32)).astype(bf16)

        def fold(values):
            return jnp.sum(values.reshape(BLOCK // 8, 8, BLOCK), axis=0)

        def tile(entry, share):
            at = pos_ref[slot, entry]
            rows = pl.ds(pl.multiple_of(at * BLOCK, BLOCK), BLOCK)
            key = kv[rows, 0:HEAD_DIM]
            value = kv[rows, HEAD_DIM : 2 * HEAD_DIM]
            spread = query_stamps - stamps_ref[pl.ds(blk_ref[slot, entry], 1), :].astype(f32)
            half = nt_dot(query, key) * (0.5 * SCALE) + half_bias(spread, bias_ref)
            prob_grad = nt_dot(grad, value)
            th = jnp.tanh(half)
            up = 1.0 + th
            weights = (half * up * share).astype(bf16)
            slope = up * (1.0 + half * (1.0 - th))
            score_grad = prob_grad * slope * (0.5 * share)
            low = score_grad.astype(bf16)
            acc[at, 0] += nn_dot(query_t, low)
            acc[at, 1] += nn_dot(grad_t, weights)
            bias_parts = [fold(score_grad)]
            for e in range(BUCKETS - 1):
                bias_parts.append(fold(jnp.where(spread >= float(2**e), score_grad, 0.0)))
            return nn_dot(low, key), bias_parts

        def add_bias(parts):
            for c in range(BUCKETS):
                bias_acc_ref[c] += parts[c]

        total, parts = tile(0, jnp.where(causal(), inverse, 0.0))
        add_bias(parts)

        def group(step, acc_q):
            sums = None
            for j in range(BWD_GROUP):
                entry = 1 + step * BWD_GROUP + j
                valid = (entry < listed).astype(f32)
                piece, parts = tile(jnp.minimum(entry, LIST_MAX - 1), inverse * valid)
                acc_q = acc_q + piece
                sums = parts if sums is None else [a + b for a, b in zip(sums, parts)]
            add_bias(sums)
            return acc_q

        steps = (listed - 1 + BWD_GROUP - 1) // BWD_GROUP
        total = lax.fori_loop(0, steps, group, total)
        dq_ref[slot * BLOCK : (slot + 1) * BLOCK, :] = (total * SCALE).astype(bf16)
    own_acc_ref[...] = acc[0:rows_half]
    other_acc_ref[...] = acc[rows_half:].astype(bf16)


SMEM = functools.partial(pl.BlockSpec, memory_space=pltpu.SMEM)
VMEM = functools.partial(pl.BlockSpec, memory_space=pltpu.VMEM)
ANY = functools.partial(pl.BlockSpec, memory_space=pl.ANY)


def attend(pos, blk, listed, bias, stamps, query, own, other):
    return pl.pallas_call(
        attend_kernel,
        out_shape=jax.ShapeDtypeStruct((2 * BLOCK, HEAD_DIM), f32),
        in_specs=[SMEM(), SMEM(), SMEM(), SMEM(), VMEM(), VMEM(), ANY(), ANY()],
        out_specs=VMEM(),
        scratch_shapes=[
            pltpu.VMEM((BLOCKS * BLOCK, 2 * HEAD_DIM), bf16),
            pltpu.SemaphoreType.DMA((2,)),
        ],
        compiler_params=pltpu.CompilerParams(vmem_limit_bytes=VMEM_LIMIT),
        cost_estimate=pl.CostEstimate(
            flops=48 * 4 * BLOCK**3, bytes_accessed=3 << 20, transcendentals=48 * BLOCK**2
        ),
        name="attend",
    )(pos, blk, listed, bias, stamps, query, own, other)


def attend_grads(pos, blk, listed, bias, stamps, query, grad, own, other):
    half = BLOCKS // 2
    return pl.pallas_call(
        grads_kernel,
        out_shape=(
            jax.ShapeDtypeStruct((2 * BLOCK, HEAD_DIM), bf16),
            jax.ShapeDtypeStruct((half, 2, HEAD_DIM, BLOCK), f32),
            jax.ShapeDtypeStruct((half, 2, HEAD_DIM, BLOCK), bf16),
            jax.ShapeDtypeStruct((BUCKETS, 8, BLOCK), f32),
        ),
        in_specs=[SMEM(), SMEM(), SMEM(), SMEM(), VMEM(), VMEM(), VMEM(), ANY(), ANY()],
        out_specs=(VMEM(), VMEM(), VMEM(), VMEM()),
        scratch_shapes=[
            pltpu.VMEM((BLOCKS * BLOCK, 2 * HEAD_DIM), bf16),
            pltpu.VMEM((BLOCKS, 2, HEAD_DIM, BLOCK), f32),
            pltpu.SemaphoreType.DMA((2,)),
        ],
        compiler_params=pltpu.CompilerParams(vmem_limit_bytes=VMEM_LIMIT),
        cost_estimate=pl.CostEstimate(
            flops=48 * 10 * BLOCK**3, bytes_accessed=6 << 20, transcendentals=48 * BLOCK**2
        ),
        name="attend_grads",
    )(pos, blk, listed, bias, stamps, query, grad, own, other)


def exchange(values, axes):
    return lax.all_to_all(values, axes, split_axis=0, concat_axis=0, tiled=True)


def to_all(values, axes, count):
    return exchange(jnp.broadcast_to(values[None], (count,) + values.shape), axes)


def swap_core(values):
    return lax.ppermute(values, "core", [(0, 1), (1, 0)])


def body(projected, cotangent, out_weight, time_bias, block_lists, stamps):
    tokens = projected.shape[1]
    x, zh, core = lax.axis_index("x"), lax.axis_index("zh"), lax.axis_index("core")
    run = (x * 2 + zh) * 2 + core

    all_weight = lax.all_gather(out_weight, "head", axis=0, tiled=True)

    by_head = projected[0].reshape(tokens, 4, HEADS, HEAD_DIM).transpose(2, 0, 1, 3)
    by_head = by_head.reshape(HEADS, tokens, 4 * HEAD_DIM)
    got = exchange(jnp.concatenate([by_head, by_head], 0), ZLINE)
    pairs = got[:, :, HEAD_DIM : 3 * HEAD_DIM].reshape(4 * BLOCK, 2 * HEAD_DIM)
    own_run = lax.dynamic_slice_in_dim(got, zh * HEADS, HEADS, 0).reshape(2 * BLOCK, 4 * HEAD_DIM)
    query = own_run[:, :HEAD_DIM]
    gate = own_run[:, 3 * HEAD_DIM :].astype(f32)
    own_pairs = to_all(pairs, "x", 4).reshape(16 * BLOCK, 2 * HEAD_DIM)
    other_pairs = swap_core(own_pairs)

    lists = lax.dynamic_slice_in_dim(block_lists[0], run * 2, 2, 0)
    listed = jnp.sum((lists >= 0).astype(jnp.int32), 1)
    blk = jnp.maximum(lists, 0)
    side = ((blk // 2) % 2) ^ core
    pos = ((side * 4 + blk // 8) * 2 + (blk // 4) % 2) * 2 + blk % 2
    bias = time_bias[0]
    stamp_blocks = stamps[0].reshape(BLOCKS, BLOCK)

    attended = attend(pos, blk, listed, bias, stamp_blocks, query, own_pairs, other_pairs)

    cot = to_all(cotangent[0], "head", HEADS).reshape(2 * BLOCK, D)
    gated_grad = nt_dot(cot, out_weight)
    normed_grad = gated_grad * gate
    sums = jnp.stack(
        [
            jnp.sum(attended, 1),
            jnp.sum(attended * attended, 1),
            jnp.sum(normed_grad, 1),
            jnp.sum(normed_grad * attended, 1),
        ]
    )
    sums = jnp.sum(to_all(sums, "head", HEADS).reshape(HEADS, 4, 2 * BLOCK), 0) / D
    mean = sums[0]
    inverse = lax.rsqrt(sums[1] - mean * mean + EPS)
    first = sums[2]
    second = inverse * (sums[3] - mean * sums[2])
    normed = (attended - mean[:, None]) * inverse[:, None]
    gated = (normed * gate).astype(bf16)
    grad_u = (gated_grad * normed).astype(bf16)
    attended_grad = (
        (normed_grad - first[:, None] - normed * second[:, None]) * inverse[:, None]
    ).astype(bf16)

    weight_part = lax.dot_general(gated, cot, (((0,), (0,)), ((), ())), preferred_element_type=f32)
    weight_rows = exchange(weight_part.astype(bf16).reshape(64, 2, D), TEAM)
    weight_rows = jnp.sum(weight_rows.astype(f32), 0)
    weight_grad = to_all(weight_rows, TEAM, 64).reshape(HEAD_DIM, D)

    grad_q, own_grads, other_grads, bias_sums = attend_grads(
        pos, blk, listed, bias, stamp_blocks, query, attended_grad, own_pairs, other_pairs
    )
    reach = jnp.sum(bias_sums, (1, 2))
    bias_part = reach - jnp.concatenate([reach[1:], jnp.zeros((1,), f32)])
    bias_grad = jnp.sum(to_all(bias_part, TEAM, 64).reshape(64, 1, BUCKETS), 0)

    chip = (own_grads + swap_core(other_grads).astype(f32)).astype(bf16)
    line = exchange(chip.reshape(4, 4, 2, HEAD_DIM, BLOCK), "x")
    line = jnp.sum(line.reshape(4, 4, 2, HEAD_DIM, BLOCK).astype(f32), 0).astype(bf16)
    line = line.transpose(0, 3, 1, 2).reshape(16, tokens, 2 * HEAD_DIM)
    rows = jnp.concatenate([grad_q, grad_u, gated], 1).reshape(HEADS, tokens, 3 * HEAD_DIM)
    back = jnp.concatenate([line, jnp.concatenate([rows, rows], 0)], 2)
    back = exchange(back, ZLINE)
    pair_grads = back[:HEADS, :, : 2 * HEAD_DIM].astype(f32) + back[HEADS:, :, : 2 * HEAD_DIM]
    rows = lax.dynamic_slice_in_dim(back, zh * HEADS, HEADS, 0)[:, :, 2 * HEAD_DIM :]
    grad_k = (pair_grads[:, :, :HEAD_DIM] * SCALE).astype(bf16)
    grad_v = pair_grads[:, :, HEAD_DIM:].astype(bf16)
    grads = jnp.stack(
        [rows[:, :, :HEAD_DIM], grad_k, grad_v, rows[:, :, HEAD_DIM : 2 * HEAD_DIM]], 0
    )
    input_grads = grads.transpose(2, 0, 1, 3).reshape(1, tokens, 4, D)
    token_side = rows[:, :, 2 * HEAD_DIM :].transpose(1, 0, 2).reshape(tokens, D)
    layer_out = nn_dot(token_side, all_weight).astype(bf16).reshape(1, tokens, D)
    return (layer_out, input_grads, weight_grad, bias_grad)


def solution(mesh):
    fine = Mesh(
        mesh.devices.reshape(4, 4, 2, 2, 8), ("dp", "x", "zh", "core", "head")
    )
    run = SEQ + ("head",)
    in_specs = (
        P("dp", run, None, None),
        P("dp", run, None),
        P("head", None),
        P("head", None),
        P("dp", None, None),
        P("dp", None),
    )
    out_specs = (
        P("dp", run, None),
        P("dp", run, None, None),
        P("head", None),
        P("head", None),
    )
    return jax.shard_map(body, mesh=fine, in_specs=in_specs, out_specs=out_specs, check_vma=False)
```

```python
import functools

import jax
import jax.numpy as jnp
from jax import lax
from jax.experimental import pallas as pl
from jax.experimental.pallas import tpu as pltpu
from jax.sharding import Mesh, PartitionSpec as P

HEADS = 8
HEAD_DIM = 128
D = 1024
BLOCK = 128
BUCKETS = 16
BLOCKS = 32
LIST_MAX = 24
EPS = 1e-05
SCALE = HEAD_DIM ** (-0.5)

SEQ = ("x", "zh", "core")
ZLINE = ("zh", "head")
VMEM_LIMIT = 48 * 1024 * 1024
f32 = jnp.float32
bf16 = jnp.bfloat16

FWD_GROUP = 4
BWD_GROUP = 4
NARROW = 2
PARTS = 2
TILES = 8
SHIFTS = (1, 3, 2)


def nt_dot(a, b):
    return lax.dot_general(a, b, (((1,), (1,)), ((), ())), preferred_element_type=f32)


def nn_dot(a, b):
    return lax.dot_general(a, b, (((1,), (0,)), ((), ())), preferred_element_type=f32)


def slot_setup(slot, blk_ref, n_ref, stamps_ref):
    listed = n_ref[slot]
    block = blk_ref[slot, 0]
    row = jnp.broadcast_to(stamps_ref[pl.ds(block, 1), :].astype(f32), (BLOCK, BLOCK))
    query_stamps = jnp.transpose(row)
    within = lax.broadcasted_iota(jnp.int32, (BLOCK, BLOCK), 0)
    counts = (BLOCK * (listed - 1) + within + 1).astype(f32)
    return listed, query_stamps, 1.0 / counts


def causal():
    rows = lax.broadcasted_iota(jnp.int32, (BLOCK, BLOCK), 0)
    cols = lax.broadcasted_iota(jnp.int32, (BLOCK, BLOCK), 1)
    return cols <= rows


def steps_of(low, narrow):
    if not narrow:
        return list(range(1, BUCKETS))
    return [jnp.minimum(low + k, BUCKETS) for k in range(1, NARROW + 1)]


def half_bias(spread, low, narrow, bias_ref, power_ref):
    first = low if narrow else 0
    bias = jnp.full((BLOCK, BLOCK), bias_ref[first] * 0.5, f32)
    for c in steps_of(low, narrow):
        bias = jnp.where(spread >= power_ref[c], bias_ref[c] * 0.5, bias)
    return bias


def all_narrow(width_ref, slot, entries):
    widest = width_ref[slot, entries[0]]
    for entry in entries[1:]:
        widest = jnp.maximum(widest, width_ref[slot, entry])
    return widest <= NARROW


def load_pairs(parts, kv, sems):
    copies = []
    for k, part in enumerate(parts):
        rows = part.shape[0]
        copies.append(pltpu.make_async_copy(part, kv.at[pl.ds(k * rows, rows)], sems.at[k]))
    for copy in copies:
        copy.start()
    for copy in copies:
        copy.wait()


def attend_kernel(
    pos_ref, home_ref, blk_ref, low_ref, width_ref, n_ref, bias_ref, power_ref, stamps_ref, q_ref, *refs
):
    parts, (out_ref, kv, sems) = refs[:PARTS], refs[PARTS:]
    load_pairs(parts, kv, sems)
    for slot in range(2):
        listed, query_stamps, inverse = slot_setup(slot, blk_ref, n_ref, stamps_ref)
        query = q_ref[slot * BLOCK : (slot + 1) * BLOCK, :]

        def tile(entry, share, narrow):
            rows = pl.ds(pl.multiple_of(pos_ref[slot, entry] * BLOCK, BLOCK), BLOCK)
            key = kv[rows, 0:HEAD_DIM]
            value = kv[rows, HEAD_DIM : 2 * HEAD_DIM]
            spread = query_stamps - stamps_ref[pl.ds(blk_ref[slot, entry], 1), :].astype(f32)
            bias = half_bias(spread, low_ref[slot, entry], narrow, bias_ref, power_ref)
            half = nt_dot(query, key) * (0.5 * SCALE) + bias
            weights = ((half + half * jnp.tanh(half)) * share).astype(bf16)
            return nn_dot(weights, value)

        def run(step, acc, narrow):
            for j in range(FWD_GROUP):
                entry = 1 + step * FWD_GROUP + j
                valid = (entry < listed).astype(f32)
                acc = acc + tile(jnp.minimum(entry, LIST_MAX - 1), inverse * valid, narrow)
            return acc

        def group(step, acc):
            entries = [jnp.minimum(1 + step * FWD_GROUP + j, LIST_MAX - 1) for j in range(FWD_GROUP)]
            return lax.cond(
                all_narrow(width_ref, slot, entries),
                lambda value: run(step, value, True),
                lambda value: run(step, value, False),
                acc,
            )

        total = tile(0, jnp.where(causal(), inverse, 0.0), False)
        steps = (listed - 1 + FWD_GROUP - 1) // FWD_GROUP
        out_ref[slot * BLOCK : (slot + 1) * BLOCK, :] = lax.fori_loop(0, steps, group, total)


def grads_kernel(
    pos_ref, home_ref, blk_ref, low_ref, width_ref, n_ref, bias_ref, power_ref, stamps_ref, q_ref, g_ref, *refs
):
    parts = refs[:PARTS]
    own_ref, other_ref, dq_ref, bins_ref, kv, acc, sems = refs[PARTS:]
    acc[...] = jnp.zeros(acc.shape, f32)
    bins_ref[...] = jnp.zeros(bins_ref.shape, f32)
    load_pairs(parts, kv, sems)
    for slot in range(2):
        listed, query_stamps, inverse = slot_setup(slot, blk_ref, n_ref, stamps_ref)
        query = q_ref[slot * BLOCK : (slot + 1) * BLOCK, :]
        grad = g_ref[slot * BLOCK : (slot + 1) * BLOCK, :]
        query_t = jnp.transpose(query.astype(f32)).astype(bf16)
        grad_t = jnp.transpose(grad.astype(f32)).astype(bf16)

        def fold(values):
            return jnp.sum(values.reshape(BLOCK // 8, 8, BLOCK), axis=0)

        def tile(entry, share, narrow):
            at = home_ref[slot, entry]
            low = low_ref[slot, entry]
            rows = pl.ds(pl.multiple_of(pos_ref[slot, entry] * BLOCK, BLOCK), BLOCK)
            key = kv[rows, 0:HEAD_DIM]
            value = kv[rows, HEAD_DIM : 2 * HEAD_DIM]
            spread = query_stamps - stamps_ref[pl.ds(blk_ref[slot, entry], 1), :].astype(f32)
            bias = half_bias(spread, low, narrow, bias_ref, power_ref)
            half = nt_dot(query, key) * (0.5 * SCALE) + bias
            prob_grad = nt_dot(grad, value)
            th = jnp.tanh(half)
            up = 1.0 + th
            weights = (half * up * share).astype(bf16)
            score_grad = prob_grad * (up * (1.0 + half * (1.0 - th))) * (0.5 * share)
            rounded = score_grad.astype(bf16)
            acc[at, 0] += nn_dot(query_t, rounded)
            acc[at, 1] += nn_dot(grad_t, weights)
            above = fold(score_grad)
            before = low if narrow else 0
            for c in steps_of(low, narrow):
                reach = fold(jnp.where(spread >= power_ref[c], score_grad, 0.0))
                bins_ref[before] += above - reach
                above, before = reach, c
            bins_ref[before] += above
            return nn_dot(rounded, key)

        def run(step, acc_q, narrow):
            for j in range(BWD_GROUP):
                entry = 1 + step * BWD_GROUP + j
                valid = (entry < listed).astype(f32)
                acc_q = acc_q + tile(jnp.minimum(entry, LIST_MAX - 1), inverse * valid, narrow)
            return acc_q

        def group(step, acc_q):
            entries = [jnp.minimum(1 + step * BWD_GROUP + j, LIST_MAX - 1) for j in range(BWD_GROUP)]
            return lax.cond(
                all_narrow(width_ref, slot, entries),
                lambda value: run(step, value, True),
                lambda value: run(step, value, False),
                acc_q,
            )

        total = tile(0, jnp.where(causal(), inverse, 0.0), False)
        steps = (listed - 1 + BWD_GROUP - 1) // BWD_GROUP
        total = lax.fori_loop(0, steps, group, total)
        dq_ref[slot * BLOCK : (slot + 1) * BLOCK, :] = (total * SCALE).astype(bf16)
    half = BLOCKS // 2
    own_ref[...] = acc[0:half].reshape(own_ref.shape)
    other_ref[0 : 4 * TILES] = acc[half:].reshape(own_ref.shape).astype(bf16)
    bins = jnp.sum(bins_ref[0:BUCKETS], axis=1)
    high = bins.astype(bf16)
    low = (bins - high.astype(f32)).astype(bf16)
    rest = jnp.zeros((BLOCK - 2 * BUCKETS, BLOCK), bf16)
    other_ref[4 * TILES] = jnp.concatenate([high, low, rest], 0)


SMEM = functools.partial(pl.BlockSpec, memory_space=pltpu.SMEM)
VMEM = functools.partial(pl.BlockSpec, memory_space=pltpu.VMEM)
ANY = functools.partial(pl.BlockSpec, memory_space=pl.ANY)


def attend(tables, query, parts):
    return pl.pallas_call(
        attend_kernel,
        out_shape=jax.ShapeDtypeStruct((2 * BLOCK, HEAD_DIM), f32),
        in_specs=[SMEM()] * 8 + [VMEM()] * 2 + [ANY()] * PARTS,
        out_specs=VMEM(),
        scratch_shapes=[
            pltpu.VMEM((BLOCKS * BLOCK, 2 * HEAD_DIM), bf16),
            pltpu.SemaphoreType.DMA((PARTS,)),
        ],
        compiler_params=pltpu.CompilerParams(vmem_limit_bytes=VMEM_LIMIT),
        cost_estimate=pl.CostEstimate(
            flops=5 * 10**9, bytes_accessed=3 << 20, transcendentals=48 * BLOCK**2
        ),
        name="attend",
    )(*tables, query, *parts)


def attend_grads(tables, query, grad, parts):
    return pl.pallas_call(
        grads_kernel,
        out_shape=(
            jax.ShapeDtypeStruct((4 * TILES, HEAD_DIM, BLOCK), f32),
            jax.ShapeDtypeStruct((4 * TILES + 1, HEAD_DIM, BLOCK), bf16),
            jax.ShapeDtypeStruct((2 * BLOCK, HEAD_DIM), bf16),
            jax.ShapeDtypeStruct((BUCKETS + 1, 8, BLOCK), f32),
        ),
        in_specs=[SMEM()] * 8 + [VMEM()] * 3 + [ANY()] * PARTS,
        out_specs=(VMEM(),) * 4,
        scratch_shapes=[
            pltpu.VMEM((BLOCKS * BLOCK, 2 * HEAD_DIM), bf16),
            pltpu.VMEM((BLOCKS, 2, HEAD_DIM, BLOCK), f32),
            pltpu.SemaphoreType.DMA((PARTS,)),
        ],
        compiler_params=pltpu.CompilerParams(vmem_limit_bytes=VMEM_LIMIT),
        cost_estimate=pl.CostEstimate(
            flops=12 * 10**9, bytes_accessed=6 << 20, transcendentals=48 * BLOCK**2
        ),
        name="attend_grads",
    )(*tables, query, grad, *parts)


def exchange(values, axes):
    return lax.all_to_all(values, axes, split_axis=0, concat_axis=0, tiled=True)


def to_all(values, axes, count):
    return exchange(jnp.broadcast_to(values[None], (count,) + values.shape), axes)


def swap_core(values):
    return lax.ppermute(values, "core", [(0, 1), (1, 0)])


def shift_x(values, by):
    return lax.ppermute(values, "x", [(i, (i + by) % 4) for i in range(4)])


def flip(values, axis, by):
    return lax.ppermute(values, axis, [(i, i ^ by) for i in range(lax.axis_size(axis))])


def after(values, *others):
    return lax.optimization_barrier((values,) + others)[0]


def joined(values, theirs, axis, by):
    late = (lax.axis_index(axis) & by) != 0
    return jnp.concatenate([jnp.where(late, theirs, values), jnp.where(late, values, theirs)], 1)


def halves(bias):
    high = lax.reduce_precision(bias, exponent_bits=8, mantissa_bits=7)
    return jnp.pad(jnp.stack([high, bias - high]), ((0, 14), (0, BLOCK - BUCKETS)))


def whole(rows):
    return rows[0, :BUCKETS] + rows[1, :BUCKETS]


def tables_of(lists, blk, pos, home, run, stamp_blocks, time_bias):
    listed = jnp.sum((lists >= 0).astype(jnp.int32), 1)
    powers = 2 ** jnp.arange(BUCKETS - 1, dtype=jnp.int32)
    own = lax.dynamic_slice_in_dim(stamp_blocks, run * 2, 2, 0)
    first = stamp_blocks[:, 0][blk]
    last = stamp_blocks[:, BLOCK - 1][blk]
    least = jnp.maximum(own[:, :1] - last, 0)
    most = own[:, BLOCK - 1 :] - first
    low = jnp.sum((least[:, :, None] >= powers).astype(jnp.int32), -1)
    high = jnp.sum((most[:, :, None] >= powers).astype(jnp.int32), -1)
    bias = jnp.concatenate([time_bias, jnp.zeros((1,), f32)])
    limits = jnp.concatenate([jnp.zeros((1,), jnp.int32), powers, jnp.full((1,), 1 << 30)])
    return (pos, home, blk, low, high - low, listed, bias, limits.astype(f32), stamp_blocks)


def body(projected, cotangent, out_weight, time_bias, block_lists, stamps):
    tokens = projected.shape[1]
    x, zh, core = lax.axis_index("x"), lax.axis_index("zh"), lax.axis_index("core")
    run = (x * 2 + zh) * 2 + core

    by_head = projected[0].reshape(tokens, 4, HEADS, HEAD_DIM).transpose(2, 0, 1, 3)
    pairs = by_head[:, :, 1:3].reshape(HEADS, tokens, 2 * HEAD_DIM)
    pairs = exchange(jnp.concatenate([pairs, pairs], 0), ZLINE).reshape(4 * BLOCK, 2 * HEAD_DIM)
    dp = lax.axis_index("dp")
    slab = lax.dynamic_slice(out_weight, (dp * tokens, (x * 2 + core) * BLOCK), (tokens, BLOCK))
    rest = jnp.concatenate([cotangent[0], slab], 1)
    rest = jnp.broadcast_to(rest, (HEADS,) + rest.shape)
    rest = exchange(jnp.concatenate([by_head[:, :, 0], by_head[:, :, 3], rest], 2), "head")
    slabs = rest[:, :, 2 * HEAD_DIM + D :].reshape(HEADS * tokens, BLOCK)
    all_weight = lax.all_gather(slabs, ("x", "core", "dp"), axis=0, tiled=True)
    all_weight = all_weight.reshape(8, 4, HEADS, tokens, BLOCK).transpose(0, 2, 1, 3, 4)
    all_weight = all_weight.reshape(8, D, BLOCK)
    rest = rest[:, :, : 2 * HEAD_DIM + D].reshape(2 * BLOCK, 2 * HEAD_DIM + D)
    query = rest[:, :HEAD_DIM]
    gate = rest[:, HEAD_DIM : 2 * HEAD_DIM].astype(f32)
    cot = rest[:, 2 * HEAD_DIM :]
    own_pairs = jnp.concatenate([pairs] + [shift_x(pairs, by) for by in SHIFTS], 0)
    parts = [own_pairs, swap_core(own_pairs)]

    lists = lax.dynamic_slice_in_dim(block_lists[0], run * 2, 2, 0)
    blk = jnp.maximum(lists, 0)
    side = ((blk // 2) % 2) ^ core
    ahead = (x - blk // 8) & 3
    place = jnp.where(ahead == 2, 3, jnp.where(ahead == 3, 2, ahead))
    pos = ((side * 4 + place) * 2 + (blk // 4) % 2) * 2 + blk % 2
    home = ((side * 4 + blk // 8) * 2 + (blk // 4) % 2) * 2 + blk % 2
    stamp_blocks = stamps[0].reshape(BLOCKS, BLOCK)
    tables = tables_of(lists, blk, pos, home, run, stamp_blocks, time_bias[0])

    attended = attend(tables, query, parts)

    gated_grad = nt_dot(cot, out_weight)
    normed_grad = gated_grad * gate
    sums = jnp.stack(
        [
            jnp.sum(attended, 1),
            jnp.sum(attended * attended, 1),
            jnp.sum(normed_grad, 1),
            jnp.sum(normed_grad * attended, 1),
        ]
    )
    sums = jnp.sum(to_all(sums, "head", HEADS).reshape(HEADS, 4, 2 * BLOCK), 0) / D
    mean = sums[0]
    inverse = lax.rsqrt(sums[1] - mean * mean + EPS)
    first = sums[2]
    second = inverse * (sums[3] - mean * sums[2])
    normed = (attended - mean[:, None]) * inverse[:, None]
    gated = (normed * gate).astype(bf16)
    grad_u = (gated_grad * normed).astype(bf16)
    attended_grad = (
        (normed_grad - first[:, None] - normed * second[:, None]) * inverse[:, None]
    ).astype(bf16)

    weight_part = lax.dot_general(gated, cot, (((0,), (0,)), ((), ())), preferred_element_type=f32)
    weight_part = weight_part.astype(bf16).reshape(HEAD_DIM, 8, BLOCK).transpose(1, 0, 2)
    weight_part = exchange(weight_part, "dp").reshape(4, 2, HEAD_DIM, BLOCK)

    own_grads, other_grads, grad_q, bins = attend_grads(tables, query, attended_grad, parts)
    weight_part = jnp.sum(weight_part.astype(f32), 0)
    sent = lax.dynamic_index_in_dim(weight_part, 1 - core, 0, True).astype(bf16)
    theirs = swap_core(jnp.concatenate([other_grads, sent], 0)).astype(f32)
    chip = (own_grads + theirs[: 4 * TILES]).reshape(4, TILES * HEAD_DIM, BLOCK)
    weight_part = lax.dynamic_index_in_dim(weight_part, core, 0, False) + theirs[4 * TILES + 1]
    bias_part = jnp.sum(theirs[4 * TILES, : 2 * BUCKETS], 1).reshape(2, BUCKETS).sum(0)
    bias_part += jnp.sum(bins, (1, 2))[:BUCKETS]
    side = jnp.concatenate([weight_part, halves(bias_part)], 0)
    side = jnp.broadcast_to(side, (4,) + side.shape)
    chip = jnp.concatenate([chip, side], 1).astype(bf16)
    line = jnp.sum(exchange(chip, "x").reshape(chip.shape).astype(f32), 0)

    split = TILES * HEAD_DIM
    pair = line[:split].reshape(2, split // 2, BLOCK)
    own_tiles = lax.dynamic_index_in_dim(pair, zh, 0, False)
    sent = lax.dynamic_index_in_dim(pair, 1 - zh, 0, False)
    weight_part, bias_part = line[split : split + HEAD_DIM], whole(line[split + HEAD_DIM :])
    sent = jnp.concatenate([sent, weight_part, halves(bias_part)], 0).astype(bf16)
    theirs = flip(sent, "zh", 1).astype(f32)
    own_tiles = own_tiles + theirs[: split // 2]
    theirs = theirs[split // 2 :]
    columns = weight_part.astype(bf16).astype(f32) + theirs[:HEAD_DIM]
    bias_part = bias_part + whole(theirs[HEAD_DIM:])

    for by in (1, 2):
        sent = jnp.pad(bias_part[None], ((0, 7), (0, columns.shape[1] - BUCKETS)))
        theirs = flip(jnp.concatenate([columns, sent], 0), "dp", by)
        bias_part = bias_part + theirs[HEAD_DIM, :BUCKETS]
        columns = joined(columns, theirs[:HEAD_DIM], "dp", by)
    bias_grad = bias_part[None]
    columns = columns.reshape(HEAD_DIM, 4, BLOCK)
    theirs = swap_core(columns)
    both = jnp.stack([jnp.where(core == 0, columns, theirs), jnp.where(core == 0, theirs, columns)])
    weight_grad = both.transpose(1, 2, 0, 3).reshape(HEAD_DIM, D)

    line = own_tiles.astype(bf16).reshape(2, 2, HEAD_DIM, BLOCK)
    line = line.transpose(0, 3, 1, 2).reshape(HEADS, tokens, 2 * HEAD_DIM)
    rows = jnp.concatenate([grad_q, grad_u, gated], 1).reshape(HEADS, tokens, 3 * HEAD_DIM)
    back = exchange(jnp.concatenate([line, rows], 2), "head")
    rows = back[:, :, 2 * HEAD_DIM :]
    pair_grads = back[:, :, : 2 * HEAD_DIM].astype(f32)
    grad_k = (pair_grads[:, :, :HEAD_DIM] * SCALE).astype(bf16)
    grad_v = pair_grads[:, :, HEAD_DIM:].astype(bf16)
    grad_u = rows[:, :, HEAD_DIM : 2 * HEAD_DIM]
    grads = jnp.stack([rows[:, :, :HEAD_DIM], grad_k, grad_v, grad_u], 0)
    input_grads = grads.transpose(2, 0, 1, 3).reshape(1, tokens, 4, D)
    token_side = rows[:, :, 2 * HEAD_DIM :].transpose(1, 0, 2).reshape(tokens, D)
    layer_out = jnp.concatenate([nn_dot(token_side, all_weight[k]) for k in range(8)], 1)
    layer_out = layer_out.astype(bf16).reshape(1, tokens, D)
    return (layer_out, input_grads, weight_grad, bias_grad)


def solution(mesh):
    fine = Mesh(
        mesh.devices.reshape(4, 4, 2, 2, 8), ("dp", "x", "zh", "core", "head")
    )
    run = SEQ + ("head",)
    in_specs = (
        P("dp", run, None, None),
        P("dp", run, None),
        P("head", None),
        P("head", None),
        P("dp", None, None),
        P("dp", None),
    )
    out_specs = (
        P("dp", run, None),
        P("dp", run, None, None),
        P("head", None),
        P("head", None),
    )
    return jax.shard_map(body, mesh=fine, in_specs=in_specs, out_specs=out_specs, check_vma=False)
```

```python
import functools

import jax
import jax.numpy as jnp
from jax import lax
from jax.experimental import pallas as pl
from jax.experimental.pallas import tpu as pltpu
from jax.sharding import Mesh, PartitionSpec as P

HEADS = 8
HEAD_DIM = 128
D = 1024
BLOCK = 128
BUCKETS = 16
BLOCKS = 32
LIST_MAX = 24
EPS = 1e-05
SCALE = HEAD_DIM ** (-0.5)

SEQ = ("x", "zh", "core")
ZLINE = ("zh", "head")
MIB = 1024 * 1024
f32 = jnp.float32
bf16 = jnp.bfloat16

FWD_GROUP = 8
BWD_GROUP = 8
NARROW = 2
PARTS = 2
TILES = 8
SHIFTS = (1, 3, 2)


def nt_dot(a, b):
    return lax.dot_general(a, b, (((1,), (1,)), ((), ())), preferred_element_type=f32)


def nn_dot(a, b):
    return lax.dot_general(a, b, (((1,), (0,)), ((), ())), preferred_element_type=f32)


def slot_setup(slot, blk_ref, n_ref, stamps_ref):
    listed = n_ref[slot]
    block = blk_ref[slot, 0]
    row = jnp.broadcast_to(stamps_ref[pl.ds(block, 1), :].astype(f32), (BLOCK, BLOCK))
    query_stamps = jnp.transpose(row)
    within = lax.broadcasted_iota(jnp.int32, (BLOCK, BLOCK), 0)
    counts = (BLOCK * (listed - 1) + within + 1).astype(f32)
    return listed, query_stamps, 1.0 / counts


def causal():
    rows = lax.broadcasted_iota(jnp.int32, (BLOCK, BLOCK), 0)
    cols = lax.broadcasted_iota(jnp.int32, (BLOCK, BLOCK), 1)
    return cols <= rows


def steps_of(low, narrow):
    if not narrow:
        return list(range(1, BUCKETS))
    return [jnp.minimum(low + k, BUCKETS) for k in range(1, NARROW + 1)]


def half_bias(spread, low, narrow, bias_ref, power_ref):
    first = low if narrow else 0
    bias = jnp.full((BLOCK, BLOCK), bias_ref[first] * 0.5, f32)
    for c in steps_of(low, narrow):
        bias = jnp.where(spread >= power_ref[c], bias_ref[c] * 0.5, bias)
    return bias


def all_narrow(width_ref, slot, entries):
    widest = width_ref[slot, entries[0]]
    for entry in entries[1:]:
        widest = jnp.maximum(widest, width_ref[slot, entry])
    return widest <= NARROW


def load_pairs(parts, kv, sems):
    copies = []
    for k, part in enumerate(parts):
        rows = part.shape[0]
        copies.append(pltpu.make_async_copy(part, kv.at[pl.ds(k * rows, rows)], sems.at[k]))
    for copy in copies:
        copy.start()
    return copies


def loaded(kv, pos_ref, slot, entries):
    keys, values = [], []
    for entry in entries:
        rows = pl.ds(pl.multiple_of(pos_ref[slot, entry] * BLOCK, BLOCK), BLOCK)
        keys.append(kv[rows, 0:HEAD_DIM])
        values.append(kv[rows, HEAD_DIM : 2 * HEAD_DIM])
    return jnp.concatenate(keys, 0), jnp.concatenate(values, 0)


def members(step, count, listed, inverse):
    entries = [1 + step * count + j for j in range(count)]
    shares = [inverse * (entry < listed).astype(f32) for entry in entries]
    return [jnp.minimum(entry, LIST_MAX - 1) for entry in entries], shares


def attend_kernel(
    pos_ref, home_ref, blk_ref, low_ref, width_ref, n_ref, bias_ref, power_ref, stamps_ref, q_ref, *refs
):
    parts, (out_ref, kv, sems) = refs[:PARTS], refs[PARTS:]
    for copy in load_pairs(parts, kv, sems):
        copy.wait()
    for slot in range(2):
        listed, query_stamps, inverse = slot_setup(slot, blk_ref, n_ref, stamps_ref)
        query = q_ref[slot * BLOCK : (slot + 1) * BLOCK, :]

        def run(entries, shares, narrow):
            keys, values = loaded(kv, pos_ref, slot, entries)
            scores = nt_dot(query, keys) * (0.5 * SCALE)
            weights = []
            for j, (entry, share) in enumerate(zip(entries, shares)):
                spread = query_stamps - stamps_ref[pl.ds(blk_ref[slot, entry], 1), :].astype(f32)
                bias = half_bias(spread, low_ref[slot, entry], narrow, bias_ref, power_ref)
                half = scores[:, j * BLOCK : (j + 1) * BLOCK] + bias
                weights.append(((half + half * jnp.tanh(half)) * share).astype(bf16))
            return nn_dot(jnp.concatenate(weights, 1), values)

        def group(step, acc):
            entries, shares = members(step, FWD_GROUP, listed, inverse)
            return acc + lax.cond(
                all_narrow(width_ref, slot, entries),
                lambda: run(entries, shares, True),
                lambda: run(entries, shares, False),
            )

        total = run([0], [jnp.where(causal(), inverse, 0.0)], False)
        steps = (listed - 1 + FWD_GROUP - 1) // FWD_GROUP
        out_ref[slot * BLOCK : (slot + 1) * BLOCK, :] = lax.fori_loop(0, steps, group, total)


def grads_kernel(
    pos_ref, home_ref, blk_ref, low_ref, width_ref, n_ref, bias_ref, power_ref, stamps_ref, q_ref, g_ref, *refs
):
    parts = refs[:PARTS]
    own_ref, other_ref, dq_ref, bins_ref, kv, acc, sems = refs[PARTS:]
    copies = load_pairs(parts, kv, sems)
    acc[...] = jnp.zeros(acc.shape, f32)
    bins_ref[...] = jnp.zeros(bins_ref.shape, f32)
    for copy in copies:
        copy.wait()
    for slot in range(2):
        listed, query_stamps, inverse = slot_setup(slot, blk_ref, n_ref, stamps_ref)
        query = q_ref[slot * BLOCK : (slot + 1) * BLOCK, :]
        grad = g_ref[slot * BLOCK : (slot + 1) * BLOCK, :]
        query_t = jnp.transpose(query.astype(f32)).astype(bf16)
        grad_t = jnp.transpose(grad.astype(f32)).astype(bf16)

        def fold(values):
            return jnp.sum(values.reshape(BLOCK // 8, 8, BLOCK), axis=0)

        def run(entries, shares, narrow):
            keys, values = loaded(kv, pos_ref, slot, entries)
            scores = nt_dot(query, keys) * (0.5 * SCALE)
            prob_grads = nt_dot(grad, values)
            weights, grads = [], []
            for j, (entry, share) in enumerate(zip(entries, shares)):
                low = low_ref[slot, entry]
                spread = query_stamps - stamps_ref[pl.ds(blk_ref[slot, entry], 1), :].astype(f32)
                bias = half_bias(spread, low, narrow, bias_ref, power_ref)
                half = scores[:, j * BLOCK : (j + 1) * BLOCK] + bias
                th = jnp.tanh(half)
                up = 1.0 + th
                weights.append((half * up * share).astype(bf16))
                slope = up * (1.0 + half * (1.0 - th)) * (0.5 * share)
                score_grad = prob_grads[:, j * BLOCK : (j + 1) * BLOCK] * slope
                grads.append(score_grad.astype(bf16))
                above = fold(score_grad)
                before = low if narrow else 0
                for c in steps_of(low, narrow):
                    reach = fold(jnp.where(spread >= power_ref[c], score_grad, 0.0))
                    bins_ref[before] += above - reach
                    above, before = reach, c
                bins_ref[before] += above
            grads, weights = jnp.concatenate(grads, 1), jnp.concatenate(weights, 1)
            key_grads, value_grads = nn_dot(query_t, grads), nn_dot(grad_t, weights)
            for j, entry in enumerate(entries):
                at = home_ref[slot, entry]
                acc[at, 0] += key_grads[:, j * BLOCK : (j + 1) * BLOCK]
                acc[at, 1] += value_grads[:, j * BLOCK : (j + 1) * BLOCK]
            return nn_dot(grads, keys)

        def group(step, acc_q):
            entries, shares = members(step, BWD_GROUP, listed, inverse)
            return acc_q + lax.cond(
                all_narrow(width_ref, slot, entries),
                lambda: run(entries, shares, True),
                lambda: run(entries, shares, False),
            )

        total = run([0], [jnp.where(causal(), inverse, 0.0)], False)
        steps = (listed - 1 + BWD_GROUP - 1) // BWD_GROUP
        total = lax.fori_loop(0, steps, group, total)
        dq_ref[slot * BLOCK : (slot + 1) * BLOCK, :] = (total * SCALE).astype(bf16)
    half = BLOCKS // 2
    own_ref[...] = acc[0:half].reshape(own_ref.shape)
    other_ref[0 : 4 * TILES] = acc[half:].reshape(own_ref.shape).astype(bf16)
    bins = jnp.sum(bins_ref[0:BUCKETS], axis=1)
    high = bins.astype(bf16)
    low = (bins - high.astype(f32)).astype(bf16)
    rest = jnp.zeros((BLOCK - 2 * BUCKETS, BLOCK), bf16)
    other_ref[4 * TILES] = jnp.concatenate([high, low, rest], 0)


def column(row):
    return jnp.transpose(jnp.broadcast_to(row, (BLOCK, row.shape[1])))


def norm_kernel(
    sums_ref, attended_ref, gated_grad_ref, gate_ref, cot_ref, gated_ref, grad_u_ref, grad_ref, w_ref
):
    sums = jnp.sum(sums_ref[...], axis=0) * (1.0 / D)
    mean, power, first, product = [column(sums[k : k + 1, :]) for k in range(4)]
    inverse = lax.rsqrt(power - mean * mean + EPS)
    second = inverse * (product - mean * first)
    gate = gate_ref[...].astype(f32)
    gated_grad = gated_grad_ref[...]
    normed = (attended_ref[...] - mean) * inverse
    gated = normed * gate
    gated_ref[...] = gated.astype(bf16)
    grad_u_ref[...] = (gated_grad * normed).astype(bf16)
    grad_ref[...] = ((gated_grad * gate - first - normed * second) * inverse).astype(bf16)
    gated_t = jnp.transpose(gated).astype(bf16)
    for k in range(8):
        w_ref[k] = nn_dot(gated_t, cot_ref[:, k * BLOCK : (k + 1) * BLOCK]).astype(bf16)


def chip_kernel(own_ref, other_ref, weight_ref, bins_ref, out_ref):
    split = TILES * HEAD_DIM
    weight = jnp.sum(weight_ref[...].astype(f32), axis=0).astype(bf16)
    tail = other_ref[4 * TILES].astype(f32)
    bins = jnp.sum(bins_ref[0:BUCKETS], axis=1)
    bins = bins + tail[0:BUCKETS] + tail[BUCKETS : 2 * BUCKETS]
    high = bins.astype(bf16)
    low = (bins - high.astype(f32)).astype(bf16)
    for k in range(4):
        for j in range(TILES):
            tile = own_ref[k * TILES + j] + other_ref[k * TILES + j].astype(f32)
            out_ref[k, j * HEAD_DIM : (j + 1) * HEAD_DIM] = tile.astype(bf16)
        out_ref[k, split : split + HEAD_DIM] = weight
        out_ref[k, split + HEAD_DIM : split + HEAD_DIM + BUCKETS] = high
        out_ref[k, split + HEAD_DIM + BUCKETS : split + HEAD_DIM + 2 * BUCKETS] = low


def project_kernel(back_ref, weight_ref, out_ref):
    gated = jnp.concatenate([back_ref[h, :, 4 * HEAD_DIM :] for h in range(HEADS)], 1)
    for k in range(8):
        rows = [weight_ref[k, d, h] for h in range(HEADS) for d in range(4)]
        product = nn_dot(gated, jnp.concatenate(rows, 0))
        out_ref[:, k * BLOCK : (k + 1) * BLOCK] = product.astype(bf16)


SMEM = functools.partial(pl.BlockSpec, memory_space=pltpu.SMEM)
VMEM = functools.partial(pl.BlockSpec, memory_space=pltpu.VMEM)
ANY = functools.partial(pl.BlockSpec, memory_space=pl.ANY)


def attend(tables, query, parts):
    return pl.pallas_call(
        attend_kernel,
        out_shape=jax.ShapeDtypeStruct((2 * BLOCK, HEAD_DIM), f32),
        in_specs=[SMEM()] * 8 + [VMEM()] * 2 + [ANY()] * PARTS,
        out_specs=VMEM(),
        scratch_shapes=[
            pltpu.VMEM((BLOCKS * BLOCK, 2 * HEAD_DIM), bf16),
            pltpu.SemaphoreType.DMA((PARTS,)),
        ],
        compiler_params=pltpu.CompilerParams(vmem_limit_bytes=12 * MIB),
        cost_estimate=pl.CostEstimate(
            flops=5 * 10**9, bytes_accessed=3 << 20, transcendentals=48 * BLOCK**2
        ),
        name="attend",
    )(*tables, query, *parts)


def attend_grads(tables, query, grad, parts):
    return pl.pallas_call(
        grads_kernel,
        out_shape=(
            jax.ShapeDtypeStruct((4 * TILES, HEAD_DIM, BLOCK), f32),
            jax.ShapeDtypeStruct((4 * TILES + 1, HEAD_DIM, BLOCK), bf16),
            jax.ShapeDtypeStruct((2 * BLOCK, HEAD_DIM), bf16),
            jax.ShapeDtypeStruct((BUCKETS + 1, 8, BLOCK), f32),
        ),
        in_specs=[SMEM()] * 8 + [VMEM()] * 3 + [ANY()] * PARTS,
        out_specs=(VMEM(),) * 4,
        scratch_shapes=[
            pltpu.VMEM((BLOCKS * BLOCK, 2 * HEAD_DIM), bf16),
            pltpu.VMEM((BLOCKS, 2, HEAD_DIM, BLOCK), f32),
            pltpu.SemaphoreType.DMA((PARTS,)),
        ],
        compiler_params=pltpu.CompilerParams(vmem_limit_bytes=24 * MIB),
        cost_estimate=pl.CostEstimate(
            flops=12 * 10**9, bytes_accessed=6 << 20, transcendentals=48 * BLOCK**2
        ),
        name="attend_grads",
    )(*tables, query, grad, *parts)


def whole_call(kernel, out_shape, name, *args):
    return pl.pallas_call(
        kernel,
        out_shape=out_shape,
        in_specs=[VMEM()] * len(args),
        out_specs=jax.tree.map(lambda _: VMEM(), out_shape),
        compiler_params=pltpu.CompilerParams(vmem_limit_bytes=12 * MIB),
        cost_estimate=pl.CostEstimate(flops=10**9, bytes_accessed=4 * MIB, transcendentals=0),
        name=name,
    )(*args)


def exchange(values, axes):
    return lax.all_to_all(values, axes, split_axis=0, concat_axis=0, tiled=True)


def to_all(values, axes, count):
    return exchange(jnp.broadcast_to(values[None], (count,) + values.shape), axes)


def swap_core(values):
    return lax.ppermute(values, "core", [(0, 1), (1, 0)])


def shift_x(values, by):
    return lax.ppermute(values, "x", [(i, (i + by) % 4) for i in range(4)])


def flip(values, axis, by):
    return lax.ppermute(values, axis, [(i, i ^ by) for i in range(lax.axis_size(axis))])


def after(values, *others):
    return lax.optimization_barrier((values,) + others)[0]


def joined(values, theirs, axis, by):
    late = (lax.axis_index(axis) & by) != 0
    return jnp.concatenate([jnp.where(late, theirs, values), jnp.where(late, values, theirs)], 1)


def halves(bias):
    high = lax.reduce_precision(bias, exponent_bits=8, mantissa_bits=7)
    return jnp.concatenate([high, bias - high], 0)


def whole(rows):
    return rows[:BUCKETS] + rows[BUCKETS:]


def tables_of(lists, blk, pos, home, run, stamp_blocks, time_bias):
    listed = jnp.sum((lists >= 0).astype(jnp.int32), 1)
    powers = 2 ** jnp.arange(BUCKETS - 1, dtype=jnp.int32)
    own = lax.dynamic_slice_in_dim(stamp_blocks, run * 2, 2, 0)
    first = stamp_blocks[:, 0][blk]
    last = stamp_blocks[:, BLOCK - 1][blk]
    least = jnp.maximum(own[:, :1] - last, 0)
    most = own[:, BLOCK - 1 :] - first
    low = jnp.sum((least[:, :, None] >= powers).astype(jnp.int32), -1)
    high = jnp.sum((most[:, :, None] >= powers).astype(jnp.int32), -1)
    bias = jnp.concatenate([time_bias, jnp.zeros((1,), f32)])
    limits = jnp.concatenate([jnp.zeros((1,), jnp.int32), powers, jnp.full((1,), 1 << 30)])
    return (pos, home, blk, low, high - low, listed, bias, limits.astype(f32), stamp_blocks)


def body(projected, cotangent, out_weight, time_bias, block_lists, stamps):
    tokens = projected.shape[1]
    x, zh, core = lax.axis_index("x"), lax.axis_index("zh"), lax.axis_index("core")
    run = (x * 2 + zh) * 2 + core

    by_head = projected[0].reshape(tokens, 4, HEADS, HEAD_DIM).transpose(2, 0, 1, 3)
    pairs = by_head[:, :, 1:3].reshape(HEADS, tokens, 2 * HEAD_DIM)
    pairs = exchange(jnp.concatenate([pairs, pairs], 0), ZLINE).reshape(4 * BLOCK, 2 * HEAD_DIM)
    dp = lax.axis_index("dp")
    slab = lax.dynamic_slice(out_weight, (dp * tokens, (x * 2 + core) * BLOCK), (tokens, BLOCK))
    rest = jnp.concatenate([cotangent[0], slab], 1)
    rest = jnp.broadcast_to(rest, (HEADS,) + rest.shape)
    rest = exchange(jnp.concatenate([by_head[:, :, 0], by_head[:, :, 3], rest], 2), "head")
    slabs = rest[:, :, 2 * HEAD_DIM + D :].reshape(HEADS * tokens, BLOCK)
    all_weight = lax.all_gather(slabs, ("x", "core", "dp"), axis=0, tiled=True)
    all_weight = all_weight.reshape(8, 4, HEADS, tokens, BLOCK)
    rest = rest[:, :, : 2 * HEAD_DIM + D].reshape(2 * BLOCK, 2 * HEAD_DIM + D)
    query = rest[:, :HEAD_DIM]
    gate = rest[:, HEAD_DIM : 2 * HEAD_DIM]
    cot = rest[:, 2 * HEAD_DIM :]
    own_pairs = jnp.concatenate([pairs] + [shift_x(pairs, by) for by in SHIFTS], 0)
    parts = [own_pairs, swap_core(own_pairs)]

    lists = lax.dynamic_slice_in_dim(block_lists[0], run * 2, 2, 0)
    blk = jnp.maximum(lists, 0)
    side = ((blk // 2) % 2) ^ core
    ahead = (x - blk // 8) & 3
    place = jnp.where(ahead == 2, 3, jnp.where(ahead == 3, 2, ahead))
    pos = ((side * 4 + place) * 2 + (blk // 4) % 2) * 2 + blk % 2
    home = ((side * 4 + blk // 8) * 2 + (blk // 4) % 2) * 2 + blk % 2
    stamp_blocks = stamps[0].reshape(BLOCKS, BLOCK)
    tables = tables_of(lists, blk, pos, home, run, stamp_blocks, time_bias[0])

    attended = attend(tables, query, parts)

    gated_grad = nt_dot(cot, out_weight)
    normed_grad = gated_grad * gate.astype(f32)
    sums = jnp.stack(
        [
            jnp.sum(attended, 1),
            jnp.sum(attended * attended, 1),
            jnp.sum(normed_grad, 1),
            jnp.sum(normed_grad * attended, 1),
        ]
    )
    sums = to_all(sums, "head", HEADS).reshape(HEADS, 4, 2 * BLOCK)
    rows = jax.ShapeDtypeStruct((2 * BLOCK, HEAD_DIM), bf16)
    tiles = jax.ShapeDtypeStruct((8, HEAD_DIM, BLOCK), bf16)
    gated, grad_u, attended_grad, weight_part = whole_call(
        norm_kernel, (rows, rows, rows, tiles), "norm", sums, attended, gated_grad, gate, cot
    )
    weight_part = exchange(weight_part, ("core", "dp"))

    own_grads, other_grads, grad_q, bins = attend_grads(tables, query, attended_grad, parts)
    theirs = swap_core(other_grads)
    split = TILES * HEAD_DIM
    chip = jax.ShapeDtypeStruct((4, split + HEAD_DIM + 2 * BUCKETS, BLOCK), bf16)
    chip = whole_call(chip_kernel, chip, "chip", own_grads, theirs, weight_part, bins)
    line = jnp.sum(exchange(chip, "x").reshape(chip.shape).astype(f32), 0)

    pair = line[:split].reshape(2, split // 2, BLOCK)
    own_tiles = lax.dynamic_index_in_dim(pair, zh, 0, False)
    sent = lax.dynamic_index_in_dim(pair, 1 - zh, 0, False)
    weight_part, bias_part = line[split : split + HEAD_DIM], whole(line[split + HEAD_DIM :])
    sent = jnp.concatenate([sent, weight_part, halves(bias_part)], 0).astype(bf16)
    theirs = flip(sent, "zh", 1).astype(f32)
    own_tiles = own_tiles + theirs[: split // 2]
    theirs = theirs[split // 2 :]
    columns = weight_part.astype(bf16).astype(f32) + theirs[:HEAD_DIM]
    bias_part = jnp.sum(bias_part + whole(theirs[HEAD_DIM:]), 1)

    for by in (1, 2):
        sent = jnp.pad(bias_part[None], ((0, 7), (0, columns.shape[1] - BUCKETS)))
        theirs = flip(jnp.concatenate([columns, sent], 0), "dp", by)
        bias_part = bias_part + theirs[HEAD_DIM, :BUCKETS]
        columns = joined(columns, theirs[:HEAD_DIM], "dp", by)
    bias_grad = bias_part[None]
    weight_grad = joined(columns, swap_core(columns), "core", 1)

    line = own_tiles.astype(bf16).reshape(2, 2, HEAD_DIM, BLOCK)
    line = line.transpose(0, 3, 1, 2).reshape(HEADS, tokens, 2 * HEAD_DIM)
    rows = jnp.concatenate([grad_q, grad_u, gated], 1).reshape(HEADS, tokens, 3 * HEAD_DIM)
    back = exchange(jnp.concatenate([line, rows], 2), "head")
    rows = back[:, :, 2 * HEAD_DIM :]
    pair_grads = back[:, :, : 2 * HEAD_DIM].astype(f32)
    grad_k = (pair_grads[:, :, :HEAD_DIM] * SCALE).astype(bf16)
    grad_v = pair_grads[:, :, HEAD_DIM:].astype(bf16)
    grad_u = rows[:, :, HEAD_DIM : 2 * HEAD_DIM]
    grads = jnp.stack([rows[:, :, :HEAD_DIM], grad_k, grad_v, grad_u], 0)
    input_grads = grads.transpose(2, 0, 1, 3).reshape(1, tokens, 4, D)
    layer_out = jax.ShapeDtypeStruct((tokens, D), bf16)
    layer_out = whole_call(project_kernel, layer_out, "project", back, all_weight)
    layer_out = layer_out.reshape(1, tokens, D)
    return (layer_out, input_grads, weight_grad, bias_grad)


def solution(mesh):
    fine = Mesh(
        mesh.devices.reshape(4, 4, 2, 2, 8), ("dp", "x", "zh", "core", "head")
    )
    run = SEQ + ("head",)
    in_specs = (
        P("dp", run, None, None),
        P("dp", run, None),
        P("head", None),
        P("head", None),
        P("dp", None, None),
        P("dp", None),
    )
    out_specs = (
        P("dp", run, None),
        P("dp", run, None, None),
        P("head", None),
        P("head", None),
    )
    return jax.shard_map(body, mesh=fine, in_specs=in_specs, out_specs=out_specs, check_vma=False)
```

```python
import functools

import jax
import jax.numpy as jnp
from jax import lax
from jax.experimental import pallas as pl
from jax.experimental.pallas import tpu as pltpu
from jax.sharding import Mesh, PartitionSpec as P

HEADS = 8
HEAD_DIM = 128
D = 1024
BLOCK = 128
BUCKETS = 16
BLOCKS = 32
LIST_MAX = 24
EPS = 1e-05
SCALE = HEAD_DIM ** (-0.5)

SEQ = ("x", "zh", "core")
ZLINE = ("zh", "head")
MIB = 1024 * 1024
f32 = jnp.float32
bf16 = jnp.bfloat16

FWD_GROUP = 8
BWD_GROUP = 8
NARROW = 2
PARTS = 2
TILES = 8
SHIFTS = (1, 3, 2)


def nt_dot(a, b):
    return lax.dot_general(a, b, (((1,), (1,)), ((), ())), preferred_element_type=f32)


def nn_dot(a, b):
    return lax.dot_general(a, b, (((1,), (0,)), ((), ())), preferred_element_type=f32)


def slot_setup(slot, blk_ref, n_ref, stamps_ref):
    listed = n_ref[slot]
    block = blk_ref[slot, 0]
    row = jnp.broadcast_to(stamps_ref[pl.ds(block, 1), :].astype(f32), (BLOCK, BLOCK))
    query_stamps = jnp.transpose(row)
    within = lax.broadcasted_iota(jnp.int32, (BLOCK, BLOCK), 0)
    counts = (BLOCK * (listed - 1) + within + 1).astype(f32)
    return listed, query_stamps, 1.0 / counts


def causal():
    rows = lax.broadcasted_iota(jnp.int32, (BLOCK, BLOCK), 0)
    cols = lax.broadcasted_iota(jnp.int32, (BLOCK, BLOCK), 1)
    return cols <= rows


def steps_of(low, narrow):
    if not narrow:
        return list(range(1, BUCKETS))
    return [jnp.minimum(low + k, BUCKETS) for k in range(1, NARROW + 1)]


def half_bias(spread, low, narrow, bias_ref, power_ref):
    first = low if narrow else 0
    bias = jnp.full((BLOCK, BLOCK), bias_ref[first] * 0.5, f32)
    for c in steps_of(low, narrow):
        bias = jnp.where(spread >= power_ref[c], bias_ref[c] * 0.5, bias)
    return bias


def all_narrow(width_ref, slot, entries):
    widest = width_ref[slot, entries[0]]
    for entry in entries[1:]:
        widest = jnp.maximum(widest, width_ref[slot, entry])
    return widest <= NARROW


def load_pairs(parts, kv, sems):
    copies = []
    for k, part in enumerate(parts):
        rows = part.shape[0]
        copies.append(pltpu.make_async_copy(part, kv.at[pl.ds(k * rows, rows)], sems.at[k]))
    for copy in copies:
        copy.start()
    return copies


def loaded(kv, pos_ref, slot, entries):
    keys, values = [], []
    for entry in entries:
        rows = pl.ds(pl.multiple_of(pos_ref[slot, entry] * BLOCK, BLOCK), BLOCK)
        keys.append(kv[rows, 0:HEAD_DIM])
        values.append(kv[rows, HEAD_DIM : 2 * HEAD_DIM])
    return jnp.concatenate(keys, 0), jnp.concatenate(values, 0)


def members(step, count, listed, inverse):
    entries = [1 + step * count + j for j in range(count)]
    shares = [inverse * (entry < listed).astype(f32) for entry in entries]
    return [jnp.minimum(entry, LIST_MAX - 1) for entry in entries], shares


def attend_kernel(
    pos_ref, home_ref, blk_ref, low_ref, width_ref, n_ref, bias_ref, power_ref, stamps_ref, q_ref, *refs
):
    parts, (out_ref, kv, sems) = refs[:PARTS], refs[PARTS:]
    for copy in load_pairs(parts, kv, sems):
        copy.wait()
    for slot in range(2):
        listed, query_stamps, inverse = slot_setup(slot, blk_ref, n_ref, stamps_ref)
        query = q_ref[slot * BLOCK : (slot + 1) * BLOCK, :]

        def run(entries, shares, narrow):
            keys, values = loaded(kv, pos_ref, slot, entries)
            scores = nt_dot(query, keys) * (0.5 * SCALE)
            weights = []
            for j, (entry, share) in enumerate(zip(entries, shares)):
                spread = query_stamps - stamps_ref[pl.ds(blk_ref[slot, entry], 1), :].astype(f32)
                bias = half_bias(spread, low_ref[slot, entry], narrow, bias_ref, power_ref)
                half = scores[:, j * BLOCK : (j + 1) * BLOCK] + bias
                weights.append(((half + half * jnp.tanh(half)) * share).astype(bf16))
            return nn_dot(jnp.concatenate(weights, 1), values)

        def group(step, acc):
            entries, shares = members(step, FWD_GROUP, listed, inverse)
            return acc + lax.cond(
                all_narrow(width_ref, slot, entries),
                lambda: run(entries, shares, True),
                lambda: run(entries, shares, False),
            )

        total = run([0], [jnp.where(causal(), inverse, 0.0)], False)
        steps = (listed - 1 + FWD_GROUP - 1) // FWD_GROUP
        out_ref[slot * BLOCK : (slot + 1) * BLOCK, :] = lax.fori_loop(0, steps, group, total)


def grads_kernel(
    pos_ref, home_ref, blk_ref, low_ref, width_ref, n_ref, bias_ref, power_ref, stamps_ref, q_ref, g_ref, *refs
):
    parts = refs[:PARTS]
    own_ref, other_ref, dq_ref, bins_ref, kv, acc, sems = refs[PARTS:]
    copies = load_pairs(parts, kv, sems)
    acc[...] = jnp.zeros(acc.shape, f32)
    bins_ref[...] = jnp.zeros(bins_ref.shape, f32)
    for copy in copies:
        copy.wait()
    for slot in range(2):
        listed, query_stamps, inverse = slot_setup(slot, blk_ref, n_ref, stamps_ref)
        query = q_ref[slot * BLOCK : (slot + 1) * BLOCK, :]
        grad = g_ref[slot * BLOCK : (slot + 1) * BLOCK, :]
        query_t = jnp.transpose(query.astype(f32)).astype(bf16)
        grad_t = jnp.transpose(grad.astype(f32)).astype(bf16)

        def fold(values):
            return jnp.sum(values.reshape(BLOCK // 8, 8, BLOCK), axis=0)

        def run(entries, shares, narrow):
            keys, values = loaded(kv, pos_ref, slot, entries)
            scores = nt_dot(query, keys) * (0.5 * SCALE)
            prob_grads = nt_dot(grad, values)
            weights, grads = [], []
            for j, (entry, share) in enumerate(zip(entries, shares)):
                low = low_ref[slot, entry]
                spread = query_stamps - stamps_ref[pl.ds(blk_ref[slot, entry], 1), :].astype(f32)
                bias = half_bias(spread, low, narrow, bias_ref, power_ref)
                half = scores[:, j * BLOCK : (j + 1) * BLOCK] + bias
                th = jnp.tanh(half)
                up = 1.0 + th
                weights.append((half * up * share).astype(bf16))
                slope = up * (1.0 + half * (1.0 - th)) * (0.5 * share)
                score_grad = prob_grads[:, j * BLOCK : (j + 1) * BLOCK] * slope
                grads.append(score_grad.astype(bf16))
                above = fold(score_grad)
                before = low if narrow else 0
                for c in steps_of(low, narrow):
                    reach = fold(jnp.where(spread >= power_ref[c], score_grad, 0.0))
                    bins_ref[before] += above - reach
                    above, before = reach, c
                bins_ref[before] += above
            grads, weights = jnp.concatenate(grads, 1), jnp.concatenate(weights, 1)
            key_grads, value_grads = nn_dot(query_t, grads), nn_dot(grad_t, weights)
            for j, entry in enumerate(entries):
                at = home_ref[slot, entry]
                acc[at, 0] += key_grads[:, j * BLOCK : (j + 1) * BLOCK]
                acc[at, 1] += value_grads[:, j * BLOCK : (j + 1) * BLOCK]
            return nn_dot(grads, keys)

        def group(step, acc_q):
            entries, shares = members(step, BWD_GROUP, listed, inverse)
            return acc_q + lax.cond(
                all_narrow(width_ref, slot, entries),
                lambda: run(entries, shares, True),
                lambda: run(entries, shares, False),
            )

        total = run([0], [jnp.where(causal(), inverse, 0.0)], False)
        steps = (listed - 1 + BWD_GROUP - 1) // BWD_GROUP
        total = lax.fori_loop(0, steps, group, total)
        dq_ref[slot * BLOCK : (slot + 1) * BLOCK, :] = (total * SCALE).astype(bf16)
    half = BLOCKS // 2
    own_ref[...] = acc[0:half].reshape(own_ref.shape)
    other_ref[0 : 4 * TILES] = acc[half:].reshape(own_ref.shape).astype(bf16)
    bins = jnp.sum(bins_ref[0:BUCKETS], axis=1)
    high = bins.astype(bf16)
    low = (bins - high.astype(f32)).astype(bf16)
    rest = jnp.zeros((BLOCK - 2 * BUCKETS, BLOCK), bf16)
    other_ref[4 * TILES] = jnp.concatenate([high, low, rest], 0)


def column(row):
    return jnp.transpose(jnp.broadcast_to(row, (BLOCK, row.shape[1])))


def norm_kernel(
    sums_ref, attended_ref, gated_grad_ref, gate_ref, cot_ref, gated_ref, grad_u_ref, grad_ref, w_ref
):
    sums = jnp.sum(sums_ref[...], axis=0) * (1.0 / D)
    mean, power, first, product = [column(sums[k : k + 1, :]) for k in range(4)]
    inverse = lax.rsqrt(power - mean * mean + EPS)
    second = inverse * (product - mean * first)
    gate = gate_ref[...].astype(f32)
    gated_grad = gated_grad_ref[...]
    normed = (attended_ref[...] - mean) * inverse
    gated = normed * gate
    gated_ref[...] = gated.astype(bf16)
    grad_u_ref[...] = (gated_grad * normed).astype(bf16)
    grad_ref[...] = ((gated_grad * gate - first - normed * second) * inverse).astype(bf16)
    gated_t = jnp.transpose(gated).astype(bf16)
    for k in range(8):
        w_ref[k] = nn_dot(gated_t, cot_ref[:, k * BLOCK : (k + 1) * BLOCK]).astype(bf16)


def chip_kernel(own_ref, other_ref, weight_ref, bins_ref, out_ref):
    split = TILES * HEAD_DIM
    weight = jnp.sum(weight_ref[...].astype(f32), axis=0).astype(bf16)
    tail = other_ref[4 * TILES].astype(f32)
    bins = jnp.sum(bins_ref[0:BUCKETS], axis=1)
    bins = bins + tail[0:BUCKETS] + tail[BUCKETS : 2 * BUCKETS]
    high = bins.astype(bf16)
    low = (bins - high.astype(f32)).astype(bf16)
    for k in range(4):
        for j in range(TILES):
            tile = own_ref[k * TILES + j] + other_ref[k * TILES + j].astype(f32)
            out_ref[k, j * HEAD_DIM : (j + 1) * HEAD_DIM] = tile.astype(bf16)
        out_ref[k, split : split + HEAD_DIM] = weight
        out_ref[k, split + HEAD_DIM : split + HEAD_DIM + BUCKETS] = high
        out_ref[k, split + HEAD_DIM + BUCKETS : split + HEAD_DIM + 2 * BUCKETS] = low


def project_kernel(back_ref, weight_ref, out_ref):
    gated = jnp.concatenate([back_ref[h, :, 4 * HEAD_DIM :] for h in range(HEADS)], 1)
    for k in range(8):
        rows = [weight_ref[k, d, h] for h in range(HEADS) for d in range(4)]
        product = nn_dot(gated, jnp.concatenate(rows, 0))
        out_ref[:, k * BLOCK : (k + 1) * BLOCK] = product.astype(bf16)


SMEM = functools.partial(pl.BlockSpec, memory_space=pltpu.SMEM)
VMEM = functools.partial(pl.BlockSpec, memory_space=pltpu.VMEM)
ANY = functools.partial(pl.BlockSpec, memory_space=pl.ANY)


def attend(tables, query, parts):
    return pl.pallas_call(
        attend_kernel,
        out_shape=jax.ShapeDtypeStruct((2 * BLOCK, HEAD_DIM), f32),
        in_specs=[SMEM()] * 8 + [VMEM()] * 2 + [ANY()] * PARTS,
        out_specs=VMEM(),
        scratch_shapes=[
            pltpu.VMEM((BLOCKS * BLOCK, 2 * HEAD_DIM), bf16),
            pltpu.SemaphoreType.DMA((PARTS,)),
        ],
        compiler_params=pltpu.CompilerParams(vmem_limit_bytes=12 * MIB),
        cost_estimate=pl.CostEstimate(
            flops=5 * 10**9, bytes_accessed=3 << 20, transcendentals=48 * BLOCK**2
        ),
        name="attend",
    )(*tables, query, *parts)


def attend_grads(tables, query, grad, parts):
    return pl.pallas_call(
        grads_kernel,
        out_shape=(
            jax.ShapeDtypeStruct((4 * TILES, HEAD_DIM, BLOCK), f32),
            jax.ShapeDtypeStruct((4 * TILES + 1, HEAD_DIM, BLOCK), bf16),
            jax.ShapeDtypeStruct((2 * BLOCK, HEAD_DIM), bf16),
            jax.ShapeDtypeStruct((BUCKETS + 1, 8, BLOCK), f32),
        ),
        in_specs=[SMEM()] * 8 + [VMEM()] * 3 + [ANY()] * PARTS,
        out_specs=(VMEM(),) * 4,
        scratch_shapes=[
            pltpu.VMEM((BLOCKS * BLOCK, 2 * HEAD_DIM), bf16),
            pltpu.VMEM((BLOCKS, 2, HEAD_DIM, BLOCK), f32),
            pltpu.SemaphoreType.DMA((PARTS,)),
        ],
        compiler_params=pltpu.CompilerParams(vmem_limit_bytes=24 * MIB),
        cost_estimate=pl.CostEstimate(
            flops=12 * 10**9, bytes_accessed=6 << 20, transcendentals=48 * BLOCK**2
        ),
        name="attend_grads",
    )(*tables, query, grad, *parts)


def whole_call(kernel, out_shape, name, *args):
    return pl.pallas_call(
        kernel,
        out_shape=out_shape,
        in_specs=[VMEM()] * len(args),
        out_specs=jax.tree.map(lambda _: VMEM(), out_shape),
        compiler_params=pltpu.CompilerParams(vmem_limit_bytes=12 * MIB),
        cost_estimate=pl.CostEstimate(flops=10**9, bytes_accessed=4 * MIB, transcendentals=0),
        name=name,
    )(*args)


def exchange(values, axes):
    return lax.all_to_all(values, axes, split_axis=0, concat_axis=0, tiled=True)


def to_all(values, axes, count):
    return exchange(jnp.broadcast_to(values[None], (count,) + values.shape), axes)


def swap_core(values):
    return lax.ppermute(values, "core", [(0, 1), (1, 0)])


def shift_x(values, by):
    return lax.ppermute(values, "x", [(i, (i + by) % 4) for i in range(4)])


def flip(values, axis, by):
    return lax.ppermute(values, axis, [(i, i ^ by) for i in range(lax.axis_size(axis))])


def after(values, *others):
    return lax.optimization_barrier((values,) + others)[0]


def joined(values, theirs, axis, by):
    late = (lax.axis_index(axis) & by) != 0
    return jnp.concatenate([jnp.where(late, theirs, values), jnp.where(late, values, theirs)], 1)


def halves(bias):
    high = lax.reduce_precision(bias, exponent_bits=8, mantissa_bits=7)
    return jnp.concatenate([high, bias - high], 0)


def whole(rows):
    return rows[:BUCKETS] + rows[BUCKETS:]


def tables_of(lists, blk, pos, home, run, stamp_blocks, time_bias):
    listed = jnp.sum((lists >= 0).astype(jnp.int32), 1)
    powers = 2 ** jnp.arange(BUCKETS - 1, dtype=jnp.int32)
    own = lax.dynamic_slice_in_dim(stamp_blocks, run * 2, 2, 0)
    first = stamp_blocks[:, 0][blk]
    last = stamp_blocks[:, BLOCK - 1][blk]
    least = jnp.maximum(own[:, :1] - last, 0)
    most = own[:, BLOCK - 1 :] - first
    low = jnp.sum((least[:, :, None] >= powers).astype(jnp.int32), -1)
    high = jnp.sum((most[:, :, None] >= powers).astype(jnp.int32), -1)
    bias = jnp.concatenate([time_bias, jnp.zeros((1,), f32)])
    limits = jnp.concatenate([jnp.zeros((1,), jnp.int32), powers, jnp.full((1,), 1 << 30)])
    return (pos, home, blk, low, high - low, listed, bias, limits.astype(f32), stamp_blocks)


def body(projected, cotangent, out_weight, time_bias, block_lists, stamps):
    tokens = projected.shape[1]
    x, zh, core = lax.axis_index("x"), lax.axis_index("zh"), lax.axis_index("core")
    run = (x * 2 + zh) * 2 + core

    by_head = projected[0].reshape(tokens, 4, HEADS, HEAD_DIM).transpose(2, 0, 1, 3)
    pairs = by_head[:, :, 1:3].reshape(HEADS, tokens, 2 * HEAD_DIM)
    pairs = exchange(jnp.concatenate([pairs, pairs], 0), ZLINE).reshape(4 * BLOCK, 2 * HEAD_DIM)
    dp = lax.axis_index("dp")
    slab = lax.dynamic_slice(out_weight, (dp * tokens, (x * 2 + core) * BLOCK), (tokens, BLOCK))
    rest = jnp.concatenate([cotangent[0], slab], 1)
    rest = jnp.broadcast_to(rest, (HEADS,) + rest.shape)
    rest = exchange(jnp.concatenate([by_head[:, :, 0], by_head[:, :, 3], rest], 2), "head")
    slabs = rest[:, :, 2 * HEAD_DIM + D :].reshape(HEADS * tokens, BLOCK)
    all_weight = lax.all_gather(slabs, ("x", "core", "dp"), axis=0, tiled=True)
    all_weight = all_weight.reshape(8, 4, HEADS, tokens, BLOCK)
    query = rest[:, :, :HEAD_DIM].reshape(2 * BLOCK, HEAD_DIM)
    gate = rest[:, :, HEAD_DIM : 2 * HEAD_DIM].reshape(2 * BLOCK, HEAD_DIM)
    cot = rest[:, :, 2 * HEAD_DIM : 2 * HEAD_DIM + D].reshape(2 * BLOCK, D)
    own_pairs = jnp.concatenate([pairs] + [shift_x(pairs, by) for by in SHIFTS], 0)
    parts = [own_pairs, swap_core(own_pairs)]

    lists = lax.dynamic_slice_in_dim(block_lists[0], run * 2, 2, 0)
    blk = jnp.maximum(lists, 0)
    side = ((blk // 2) % 2) ^ core
    ahead = (x - blk // 8) & 3
    place = jnp.where(ahead == 2, 3, jnp.where(ahead == 3, 2, ahead))
    pos = ((side * 4 + place) * 2 + (blk // 4) % 2) * 2 + blk % 2
    home = ((side * 4 + blk // 8) * 2 + (blk // 4) % 2) * 2 + blk % 2
    stamp_blocks = stamps[0].reshape(BLOCKS, BLOCK)
    tables = tables_of(lists, blk, pos, home, run, stamp_blocks, time_bias[0])

    attended = attend(tables, query, parts)

    gated_grad = nt_dot(cot, out_weight)
    normed_grad = gated_grad * gate.astype(f32)
    sums = jnp.stack(
        [
            jnp.sum(attended, 1),
            jnp.sum(attended * attended, 1),
            jnp.sum(normed_grad, 1),
            jnp.sum(normed_grad * attended, 1),
        ]
    )
    sums = to_all(sums, "head", HEADS).reshape(HEADS, 4, 2 * BLOCK)
    rows = jax.ShapeDtypeStruct((2 * BLOCK, HEAD_DIM), bf16)
    tiles = jax.ShapeDtypeStruct((8, HEAD_DIM, BLOCK), bf16)
    gated, grad_u, attended_grad, weight_part = whole_call(
        norm_kernel, (rows, rows, rows, tiles), "norm", sums, attended, gated_grad, gate, cot
    )
    weight_part = exchange(weight_part, ("core", "dp"))

    own_grads, other_grads, grad_q, bins = attend_grads(tables, query, attended_grad, parts)
    theirs = swap_core(other_grads)
    split = TILES * HEAD_DIM
    chip = jax.ShapeDtypeStruct((4, split + HEAD_DIM + 2 * BUCKETS, BLOCK), bf16)
    chip = whole_call(chip_kernel, chip, "chip", own_grads, theirs, weight_part, bins)
    line = jnp.sum(exchange(chip, "x").reshape(chip.shape).astype(f32), 0)

    pair = line[:split].reshape(2, split // 2, BLOCK)
    own_tiles = lax.dynamic_index_in_dim(pair, zh, 0, False)
    sent = lax.dynamic_index_in_dim(pair, 1 - zh, 0, False)
    weight_part, bias_part = line[split : split + HEAD_DIM], whole(line[split + HEAD_DIM :])
    sent = jnp.concatenate([sent, weight_part, halves(bias_part)], 0).astype(bf16)
    theirs = flip(sent, "zh", 1).astype(f32)
    own_tiles = own_tiles + theirs[: split // 2]
    theirs = theirs[split // 2 :]
    columns = weight_part.astype(bf16).astype(f32) + theirs[:HEAD_DIM]
    bias_part = jnp.sum(bias_part + whole(theirs[HEAD_DIM:]), 1)

    for by in (1, 2):
        sent = jnp.pad(bias_part[None], ((0, 7), (0, columns.shape[1] - BUCKETS)))
        theirs = flip(jnp.concatenate([columns, sent], 0), "dp", by)
        bias_part = bias_part + theirs[HEAD_DIM, :BUCKETS]
        columns = joined(columns, theirs[:HEAD_DIM], "dp", by)
    bias_grad = bias_part[None]
    weight_grad = joined(columns, swap_core(columns), "core", 1)

    line = own_tiles.astype(bf16).reshape(2, 2, HEAD_DIM, BLOCK)
    line = line.transpose(0, 3, 1, 2).reshape(HEADS, tokens, 2 * HEAD_DIM)
    rows = jnp.concatenate([grad_q, grad_u, gated], 1).reshape(HEADS, tokens, 3 * HEAD_DIM)
    back = exchange(jnp.concatenate([line, rows], 2), "head")
    rows = back[:, :, 2 * HEAD_DIM :]
    pair_grads = back[:, :, : 2 * HEAD_DIM].astype(f32)
    grad_k = (pair_grads[:, :, :HEAD_DIM] * SCALE).astype(bf16)
    grad_v = pair_grads[:, :, HEAD_DIM:].astype(bf16)
    grad_u = rows[:, :, HEAD_DIM : 2 * HEAD_DIM]
    grads = jnp.stack([rows[:, :, :HEAD_DIM], grad_k, grad_v, grad_u], 0)
    input_grads = grads.transpose(2, 0, 1, 3).reshape(1, tokens, 4, D)
    layer_out = jax.ShapeDtypeStruct((tokens, D), bf16)
    layer_out = whole_call(project_kernel, layer_out, "project", back, all_weight)
    layer_out = layer_out.reshape(1, tokens, D)
    return (layer_out, input_grads, weight_grad, bias_grad)


def solution(mesh):
    fine = Mesh(
        mesh.devices.reshape(4, 4, 2, 2, 8), ("dp", "x", "zh", "core", "head")
    )
    run = SEQ + ("head",)
    in_specs = (
        P("dp", run, None, None),
        P("dp", run, None),
        P("head", None),
        P("head", None),
        P("dp", None, None),
        P("dp", None),
    )
    out_specs = (
        P("dp", run, None),
        P("dp", run, None, None),
        P("head", None),
        P("head", None),
    )
    return jax.shard_map(body, mesh=fine, in_specs=in_specs, out_specs=out_specs, check_vma=False)
```

```python
import functools

import jax
import jax.numpy as jnp
from jax import lax
from jax.experimental import pallas as pl
from jax.experimental.pallas import tpu as pltpu
from jax.sharding import Mesh, PartitionSpec as P

HEADS = 8
HEAD_DIM = 128
D = 1024
BLOCK = 128
BUCKETS = 16
BLOCKS = 32
LIST_MAX = 24
EPS = 1e-05
SCALE = HEAD_DIM ** (-0.5)

SEQ = ("x", "zh", "core")
ZLINE = ("zh", "head")
MIB = 1024 * 1024
f32 = jnp.float32
bf16 = jnp.bfloat16

FWD_GROUP = 8
BWD_GROUP = 8
NARROW = 2
PARTS = 2
TILES = 8
SHIFTS = (1, 3, 2)


def nt_dot(a, b):
    return lax.dot_general(a, b, (((1,), (1,)), ((), ())), preferred_element_type=f32)


def nn_dot(a, b):
    return lax.dot_general(a, b, (((1,), (0,)), ((), ())), preferred_element_type=f32)


def slot_setup(slot, blk_ref, n_ref, stamps_ref):
    listed = n_ref[slot]
    block = blk_ref[slot, 0]
    row = jnp.broadcast_to(stamps_ref[pl.ds(block, 1), :].astype(f32), (BLOCK, BLOCK))
    query_stamps = jnp.transpose(row)
    within = lax.broadcasted_iota(jnp.int32, (BLOCK, BLOCK), 0)
    counts = (BLOCK * (listed - 1) + within + 1).astype(f32)
    return listed, query_stamps, 1.0 / counts


def causal():
    rows = lax.broadcasted_iota(jnp.int32, (BLOCK, BLOCK), 0)
    cols = lax.broadcasted_iota(jnp.int32, (BLOCK, BLOCK), 1)
    return cols <= rows


def steps_of(low, narrow):
    if not narrow:
        return list(range(1, BUCKETS))
    return [jnp.minimum(low + k, BUCKETS) for k in range(1, NARROW + 1)]


def half_bias(spread, low, narrow, bias_ref, power_ref):
    first = low if narrow else 0
    bias = jnp.full((BLOCK, BLOCK), bias_ref[first] * 0.5, f32)
    for c in steps_of(low, narrow):
        bias = jnp.where(spread >= power_ref[c], bias_ref[c] * 0.5, bias)
    return bias


def all_narrow(width_ref, slot, entries):
    widest = width_ref[slot, entries[0]]
    for entry in entries[1:]:
        widest = jnp.maximum(widest, width_ref[slot, entry])
    return widest <= NARROW


def load_pairs(parts, kv, sems):
    copies = []
    for k, part in enumerate(parts):
        rows = part.shape[0]
        copies.append(pltpu.make_async_copy(part, kv.at[pl.ds(k * rows, rows)], sems.at[k]))
    for copy in copies:
        copy.start()
    return copies


def loaded(kv, pos_ref, slot, entries):
    keys, values = [], []
    for entry in entries:
        rows = pl.ds(pl.multiple_of(pos_ref[slot, entry] * BLOCK, BLOCK), BLOCK)
        keys.append(kv[rows, 0:HEAD_DIM])
        values.append(kv[rows, HEAD_DIM : 2 * HEAD_DIM])
    return jnp.concatenate(keys, 0), jnp.concatenate(values, 0)


def members(step, count, listed, inverse):
    entries = [1 + step * count + j for j in range(count)]
    shares = [inverse * (entry < listed).astype(f32) for entry in entries]
    return [jnp.minimum(entry, LIST_MAX - 1) for entry in entries], shares


def attend_kernel(
    pos_ref, home_ref, blk_ref, low_ref, width_ref, n_ref, bias_ref, power_ref, stamps_ref, q_ref, *refs
):
    parts, (out_ref, kv, sems) = refs[:PARTS], refs[PARTS:]
    for copy in load_pairs(parts, kv, sems):
        copy.wait()
    for slot in range(2):
        listed, query_stamps, inverse = slot_setup(slot, blk_ref, n_ref, stamps_ref)
        query = q_ref[slot * BLOCK : (slot + 1) * BLOCK, :]

        def run(entries, shares, narrow):
            keys, values = loaded(kv, pos_ref, slot, entries)
            scores = nt_dot(query, keys) * (0.5 * SCALE)
            weights = []
            for j, (entry, share) in enumerate(zip(entries, shares)):
                spread = query_stamps - stamps_ref[pl.ds(blk_ref[slot, entry], 1), :].astype(f32)
                bias = half_bias(spread, low_ref[slot, entry], narrow, bias_ref, power_ref)
                half = scores[:, j * BLOCK : (j + 1) * BLOCK] + bias
                weights.append(((half + half * jnp.tanh(half)) * share).astype(bf16))
            return nn_dot(jnp.concatenate(weights, 1), values)

        def group(step, acc):
            entries, shares = members(step, FWD_GROUP, listed, inverse)
            return acc + lax.cond(
                all_narrow(width_ref, slot, entries),
                lambda: run(entries, shares, True),
                lambda: run(entries, shares, False),
            )

        total = run([0], [jnp.where(causal(), inverse, 0.0)], False)
        steps = (listed - 1 + FWD_GROUP - 1) // FWD_GROUP
        out_ref[slot * BLOCK : (slot + 1) * BLOCK, :] = lax.fori_loop(0, steps, group, total)


def grads_kernel(
    pos_ref, home_ref, blk_ref, low_ref, width_ref, n_ref, bias_ref, power_ref, stamps_ref, q_ref, g_ref, *refs
):
    kv, acc, other_ref, dq_ref, bins_ref = refs
    acc[...] = jnp.zeros(acc.shape, f32)
    bins_ref[...] = jnp.zeros(bins_ref.shape, f32)
    for slot in range(2):
        listed, query_stamps, inverse = slot_setup(slot, blk_ref, n_ref, stamps_ref)
        query = q_ref[slot * BLOCK : (slot + 1) * BLOCK, :]
        grad = g_ref[slot * BLOCK : (slot + 1) * BLOCK, :]
        query_t = jnp.transpose(query.astype(f32)).astype(bf16)
        grad_t = jnp.transpose(grad.astype(f32)).astype(bf16)

        def fold(values):
            return jnp.sum(values.reshape(BLOCK // 8, 8, BLOCK), axis=0)

        def run(entries, shares, narrow):
            keys, values = loaded(kv, pos_ref, slot, entries)
            scores = nt_dot(query, keys) * (0.5 * SCALE)
            prob_grads = nt_dot(grad, values)
            weights, grads = [], []
            for j, (entry, share) in enumerate(zip(entries, shares)):
                low = low_ref[slot, entry]
                spread = query_stamps - stamps_ref[pl.ds(blk_ref[slot, entry], 1), :].astype(f32)
                bias = half_bias(spread, low, narrow, bias_ref, power_ref)
                half = scores[:, j * BLOCK : (j + 1) * BLOCK] + bias
                th = jnp.tanh(half)
                up = 1.0 + th
                weights.append((half * up * share).astype(bf16))
                slope = up * (1.0 + half * (1.0 - th)) * (0.5 * share)
                score_grad = prob_grads[:, j * BLOCK : (j + 1) * BLOCK] * slope
                grads.append(score_grad.astype(bf16))
                above = fold(score_grad)
                before = low if narrow else 0
                for c in steps_of(low, narrow):
                    reach = fold(jnp.where(spread >= power_ref[c], score_grad, 0.0))
                    bins_ref[before] += above - reach
                    above, before = reach, c
                bins_ref[before] += above
            grads, weights = jnp.concatenate(grads, 1), jnp.concatenate(weights, 1)
            key_grads, value_grads = nn_dot(query_t, grads), nn_dot(grad_t, weights)
            for j, entry in enumerate(entries):
                at = home_ref[slot, entry]
                acc[at, 0] += key_grads[:, j * BLOCK : (j + 1) * BLOCK]
                acc[at, 1] += value_grads[:, j * BLOCK : (j + 1) * BLOCK]
            return nn_dot(grads, keys)

        def group(step, acc_q):
            entries, shares = members(step, BWD_GROUP, listed, inverse)
            return acc_q + lax.cond(
                all_narrow(width_ref, slot, entries),
                lambda: run(entries, shares, True),
                lambda: run(entries, shares, False),
            )

        total = run([0], [jnp.where(causal(), inverse, 0.0)], False)
        steps = (listed - 1 + BWD_GROUP - 1) // BWD_GROUP
        total = lax.fori_loop(0, steps, group, total)
        dq_ref[slot * BLOCK : (slot + 1) * BLOCK, :] = (total * SCALE).astype(bf16)
    half = BLOCKS // 2
    other_ref[0 : 4 * TILES] = acc[half:].reshape(4 * TILES, HEAD_DIM, BLOCK).astype(bf16)
    bins = jnp.sum(bins_ref[0:BUCKETS], axis=1)
    high = bins.astype(bf16)
    low = (bins - high.astype(f32)).astype(bf16)
    rest = jnp.zeros((BLOCK - 2 * BUCKETS, BLOCK), bf16)
    other_ref[4 * TILES] = jnp.concatenate([high, low, rest], 0)


def column(row):
    return jnp.transpose(jnp.broadcast_to(row, (BLOCK, row.shape[1])))


def norm_kernel(
    sums_ref, attended_ref, gated_grad_ref, gate_ref, cot_ref, gated_ref, grad_u_ref, grad_ref, w_ref
):
    sums = jnp.sum(sums_ref[...], axis=0) * (1.0 / D)
    mean, power, first, product = [column(sums[k : k + 1, :]) for k in range(4)]
    inverse = lax.rsqrt(power - mean * mean + EPS)
    second = inverse * (product - mean * first)
    gate = gate_ref[...].astype(f32)
    gated_grad = gated_grad_ref[...]
    normed = (attended_ref[...] - mean) * inverse
    gated = normed * gate
    gated_ref[...] = gated.astype(bf16)
    grad_u_ref[...] = (gated_grad * normed).astype(bf16)
    grad_ref[...] = ((gated_grad * gate - first - normed * second) * inverse).astype(bf16)
    gated_t = jnp.transpose(gated).astype(bf16)
    for k in range(8):
        w_ref[k] = nn_dot(gated_t, cot_ref[:, k * BLOCK : (k + 1) * BLOCK]).astype(bf16)


def chip_kernel(own_ref, other_ref, weight_ref, bins_ref, out_ref):
    split = TILES * HEAD_DIM
    weight = jnp.sum(weight_ref[...].astype(f32), axis=0).astype(bf16)
    tail = other_ref[4 * TILES].astype(f32)
    bins = jnp.sum(bins_ref[0:BUCKETS], axis=1)
    bins = bins + tail[0:BUCKETS] + tail[BUCKETS : 2 * BUCKETS]
    high = bins.astype(bf16)
    low = (bins - high.astype(f32)).astype(bf16)
    for k in range(4):
        for j in range(TILES):
            tile = own_ref[(k * TILES + j) // 2, j % 2] + other_ref[k * TILES + j].astype(f32)
            out_ref[k, j * HEAD_DIM : (j + 1) * HEAD_DIM] = tile.astype(bf16)
        out_ref[k, split : split + HEAD_DIM] = weight
        out_ref[k, split + HEAD_DIM : split + HEAD_DIM + BUCKETS] = high
        out_ref[k, split + HEAD_DIM + BUCKETS : split + HEAD_DIM + 2 * BUCKETS] = low


def project_kernel(back_ref, weight_ref, out_ref):
    gated = jnp.concatenate([back_ref[h, :, 4 * HEAD_DIM :] for h in range(HEADS)], 1)
    for k in range(8):
        rows = [weight_ref[k, d, h] for h in range(HEADS) for d in range(4)]
        product = nn_dot(gated, jnp.concatenate(rows, 0))
        out_ref[:, k * BLOCK : (k + 1) * BLOCK] = product.astype(bf16)


SMEM = functools.partial(pl.BlockSpec, memory_space=pltpu.SMEM)
VMEM = functools.partial(pl.BlockSpec, memory_space=pltpu.VMEM)
ANY = functools.partial(pl.BlockSpec, memory_space=pl.ANY)


def attend(tables, query, parts):
    return pl.pallas_call(
        attend_kernel,
        out_shape=(
            jax.ShapeDtypeStruct((2 * BLOCK, HEAD_DIM), f32),
            jax.ShapeDtypeStruct((BLOCKS * BLOCK, 2 * HEAD_DIM), bf16),
        ),
        in_specs=[SMEM()] * 8 + [VMEM()] * 2 + [ANY()] * PARTS,
        out_specs=(VMEM(), VMEM()),
        scratch_shapes=[
            pltpu.SemaphoreType.DMA((PARTS,)),
        ],
        compiler_params=pltpu.CompilerParams(vmem_limit_bytes=12 * MIB),
        cost_estimate=pl.CostEstimate(
            flops=5 * 10**9, bytes_accessed=3 << 20, transcendentals=48 * BLOCK**2
        ),
        name="attend",
    )(*tables, query, *parts)


def attend_grads(tables, query, grad, pairs):
    return pl.pallas_call(
        grads_kernel,
        out_shape=(
            jax.ShapeDtypeStruct((BLOCKS, 2, HEAD_DIM, BLOCK), f32),
            jax.ShapeDtypeStruct((4 * TILES + 1, HEAD_DIM, BLOCK), bf16),
            jax.ShapeDtypeStruct((2 * BLOCK, HEAD_DIM), bf16),
            jax.ShapeDtypeStruct((BUCKETS + 1, 8, BLOCK), f32),
        ),
        in_specs=[SMEM()] * 8 + [VMEM()] * 4,
        out_specs=(VMEM(),) * 4,
        compiler_params=pltpu.CompilerParams(vmem_limit_bytes=24 * MIB),
        cost_estimate=pl.CostEstimate(
            flops=12 * 10**9, bytes_accessed=6 << 20, transcendentals=48 * BLOCK**2
        ),
        name="attend_grads",
    )(*tables, query, grad, pairs)


def whole_call(kernel, out_shape, name, *args):
    return pl.pallas_call(
        kernel,
        out_shape=out_shape,
        in_specs=[VMEM()] * len(args),
        out_specs=jax.tree.map(lambda _: VMEM(), out_shape),
        compiler_params=pltpu.CompilerParams(vmem_limit_bytes=12 * MIB),
        cost_estimate=pl.CostEstimate(flops=10**9, bytes_accessed=4 * MIB, transcendentals=0),
        name=name,
    )(*args)


def exchange(values, axes):
    return lax.all_to_all(values, axes, split_axis=0, concat_axis=0, tiled=True)


def to_all(values, axes, count):
    return exchange(jnp.broadcast_to(values[None], (count,) + values.shape), axes)


def swap_core(values):
    return lax.ppermute(values, "core", [(0, 1), (1, 0)])


def shift_x(values, by):
    return lax.ppermute(values, "x", [(i, (i + by) % 4) for i in range(4)])


def flip(values, axis, by):
    return lax.ppermute(values, axis, [(i, i ^ by) for i in range(lax.axis_size(axis))])


def after(values, *others):
    return lax.optimization_barrier((values,) + others)[0]


def joined(values, theirs, axis, by):
    late = (lax.axis_index(axis) & by) != 0
    return jnp.concatenate([jnp.where(late, theirs, values), jnp.where(late, values, theirs)], 1)


def halves(bias):
    high = lax.reduce_precision(bias, exponent_bits=8, mantissa_bits=7)
    return jnp.concatenate([high, bias - high], 0)


def whole(rows):
    return rows[:BUCKETS] + rows[BUCKETS:]


def tables_of(lists, blk, pos, home, run, stamp_blocks, time_bias):
    listed = jnp.sum((lists >= 0).astype(jnp.int32), 1)
    powers = 2 ** jnp.arange(BUCKETS - 1, dtype=jnp.int32)
    own = lax.dynamic_slice_in_dim(stamp_blocks, run * 2, 2, 0)
    first = stamp_blocks[:, 0][blk]
    last = stamp_blocks[:, BLOCK - 1][blk]
    least = jnp.maximum(own[:, :1] - last, 0)
    most = own[:, BLOCK - 1 :] - first
    low = jnp.sum((least[:, :, None] >= powers).astype(jnp.int32), -1)
    high = jnp.sum((most[:, :, None] >= powers).astype(jnp.int32), -1)
    bias = jnp.concatenate([time_bias, jnp.zeros((1,), f32)])
    limits = jnp.concatenate([jnp.zeros((1,), jnp.int32), powers, jnp.full((1,), 1 << 30)])
    return (pos, home, blk, low, high - low, listed, bias, limits.astype(f32), stamp_blocks)


def body(projected, cotangent, out_weight, time_bias, block_lists, stamps):
    tokens = projected.shape[1]
    x, zh, core = lax.axis_index("x"), lax.axis_index("zh"), lax.axis_index("core")
    run = (x * 2 + zh) * 2 + core

    by_head = projected[0].reshape(tokens, 4, HEADS, HEAD_DIM).transpose(2, 0, 1, 3)
    pairs = by_head[:, :, 1:3].reshape(HEADS, tokens, 2 * HEAD_DIM)
    pairs = exchange(jnp.concatenate([pairs, pairs], 0), ZLINE).reshape(4 * BLOCK, 2 * HEAD_DIM)
    dp = lax.axis_index("dp")
    slab = lax.dynamic_slice(out_weight, (dp * tokens, (x * 2 + core) * BLOCK), (tokens, BLOCK))
    rest = jnp.concatenate([cotangent[0], slab], 1)
    rest = jnp.broadcast_to(rest, (HEADS,) + rest.shape)
    rest = exchange(jnp.concatenate([by_head[:, :, 0], by_head[:, :, 3], rest], 2), "head")
    slabs = rest[:, :, 2 * HEAD_DIM + D :].reshape(HEADS * tokens, BLOCK)
    all_weight = lax.all_gather(slabs, ("x", "core", "dp"), axis=0, tiled=True)
    all_weight = all_weight.reshape(8, 4, HEADS, tokens, BLOCK)
    query = rest[:, :, :HEAD_DIM].reshape(2 * BLOCK, HEAD_DIM)
    gate = rest[:, :, HEAD_DIM : 2 * HEAD_DIM].reshape(2 * BLOCK, HEAD_DIM)
    cot = rest[:, :, 2 * HEAD_DIM : 2 * HEAD_DIM + D].reshape(2 * BLOCK, D)
    own_pairs = jnp.concatenate([pairs] + [shift_x(pairs, by) for by in SHIFTS], 0)
    parts = [own_pairs, swap_core(own_pairs)]

    lists = lax.dynamic_slice_in_dim(block_lists[0], run * 2, 2, 0)
    blk = jnp.maximum(lists, 0)
    side = ((blk // 2) % 2) ^ core
    ahead = (x - blk // 8) & 3
    place = jnp.where(ahead == 2, 3, jnp.where(ahead == 3, 2, ahead))
    pos = ((side * 4 + place) * 2 + (blk // 4) % 2) * 2 + blk % 2
    home = ((side * 4 + blk // 8) * 2 + (blk // 4) % 2) * 2 + blk % 2
    stamp_blocks = stamps[0].reshape(BLOCKS, BLOCK)
    tables = tables_of(lists, blk, pos, home, run, stamp_blocks, time_bias[0])

    attended, pairs = attend(tables, query, parts)

    gated_grad = nt_dot(cot, out_weight)
    normed_grad = gated_grad * gate.astype(f32)
    sums = jnp.stack(
        [
            jnp.sum(attended, 1),
            jnp.sum(attended * attended, 1),
            jnp.sum(normed_grad, 1),
            jnp.sum(normed_grad * attended, 1),
        ]
    )
    sums = to_all(sums, "head", HEADS).reshape(HEADS, 4, 2 * BLOCK)
    rows = jax.ShapeDtypeStruct((2 * BLOCK, HEAD_DIM), bf16)
    tiles = jax.ShapeDtypeStruct((8, HEAD_DIM, BLOCK), bf16)
    gated, grad_u, attended_grad, weight_part = whole_call(
        norm_kernel, (rows, rows, rows, tiles), "norm", sums, attended, gated_grad, gate, cot
    )
    weight_part = exchange(weight_part, ("core", "dp"))

    own_grads, other_grads, grad_q, bins = attend_grads(tables, query, attended_grad, pairs)
    theirs = swap_core(other_grads)
    split = TILES * HEAD_DIM
    chip = jax.ShapeDtypeStruct((4, split + HEAD_DIM + 2 * BUCKETS, BLOCK), bf16)
    chip = whole_call(chip_kernel, chip, "chip", own_grads, theirs, weight_part, bins)
    line = jnp.sum(exchange(chip, "x").reshape(chip.shape).astype(f32), 0)

    pair = line[:split].reshape(2, split // 2, BLOCK)
    own_tiles = lax.dynamic_index_in_dim(pair, zh, 0, False)
    sent = lax.dynamic_index_in_dim(pair, 1 - zh, 0, False)
    weight_part, bias_part = line[split : split + HEAD_DIM], whole(line[split + HEAD_DIM :])
    sent = jnp.concatenate([sent, weight_part, halves(bias_part)], 0).astype(bf16)
    theirs = flip(sent, "zh", 1).astype(f32)
    own_tiles = own_tiles + theirs[: split // 2]
    theirs = theirs[split // 2 :]
    columns = weight_part.astype(bf16).astype(f32) + theirs[:HEAD_DIM]
    bias_part = jnp.sum(bias_part + whole(theirs[HEAD_DIM:]), 1)

    for by in (1, 2):
        sent = jnp.pad(bias_part[None], ((0, 7), (0, columns.shape[1] - BUCKETS)))
        theirs = flip(jnp.concatenate([columns, sent], 0), "dp", by)
        bias_part = bias_part + theirs[HEAD_DIM, :BUCKETS]
        columns = joined(columns, theirs[:HEAD_DIM], "dp", by)
    bias_grad = bias_part[None]
    weight_grad = joined(columns, swap_core(columns), "core", 1)

    line = own_tiles.astype(bf16).reshape(2, 2, HEAD_DIM, BLOCK)
    line = line.transpose(0, 3, 1, 2).reshape(HEADS, tokens, 2 * HEAD_DIM)
    rows = jnp.concatenate([grad_q, grad_u, gated], 1).reshape(HEADS, tokens, 3 * HEAD_DIM)
    back = exchange(jnp.concatenate([line, rows], 2), "head")
    rows = back[:, :, 2 * HEAD_DIM :]
    pair_grads = back[:, :, : 2 * HEAD_DIM].astype(f32)
    grad_k = (pair_grads[:, :, :HEAD_DIM] * SCALE).astype(bf16)
    grad_v = pair_grads[:, :, HEAD_DIM:].astype(bf16)
    grad_u = rows[:, :, HEAD_DIM : 2 * HEAD_DIM]
    grads = jnp.stack([rows[:, :, :HEAD_DIM], grad_k, grad_v, grad_u], 0)
    input_grads = grads.transpose(2, 0, 1, 3).reshape(1, tokens, 4, D)
    layer_out = jax.ShapeDtypeStruct((tokens, D), bf16)
    layer_out = whole_call(project_kernel, layer_out, "project", back, all_weight)
    layer_out = layer_out.reshape(1, tokens, D)
    return (layer_out, input_grads, weight_grad, bias_grad)


def solution(mesh):
    fine = Mesh(
        mesh.devices.reshape(4, 4, 2, 2, 8), ("dp", "x", "zh", "core", "head")
    )
    run = SEQ + ("head",)
    in_specs = (
        P("dp", run, None, None),
        P("dp", run, None),
        P("head", None),
        P("head", None),
        P("dp", None, None),
        P("dp", None),
    )
    out_specs = (
        P("dp", run, None),
        P("dp", run, None, None),
        P("head", None),
        P("head", None),
    )
    return jax.shard_map(body, mesh=fine, in_specs=in_specs, out_specs=out_specs, check_vma=False)
```

```python
import functools

import jax
import jax.numpy as jnp
from jax import lax
from jax.experimental import pallas as pl
from jax.experimental.pallas import tpu as pltpu
from jax.sharding import Mesh, PartitionSpec as P

HEADS = 8
HEAD_DIM = 128
D = 1024
BLOCK = 128
BUCKETS = 16
BLOCKS = 32
LIST_MAX = 24
EPS = 1e-05
SCALE = HEAD_DIM ** (-0.5)

SEQ = ("x", "zh", "core")
ZLINE = ("zh", "head")
MIB = 1024 * 1024
f32 = jnp.float32
bf16 = jnp.bfloat16

FWD_GROUP = 12
BWD_GROUP = 8
NARROW = 2
PARTS = 2
TILES = 8
SHIFTS = (1, 3, 2)


def nt_dot(a, b):
    return lax.dot_general(a, b, (((1,), (1,)), ((), ())), preferred_element_type=f32)


def nn_dot(a, b):
    return lax.dot_general(a, b, (((1,), (0,)), ((), ())), preferred_element_type=f32)


def slot_setup(slot, blk_ref, n_ref, stamps_ref):
    listed = n_ref[slot]
    block = blk_ref[slot, 0]
    row = jnp.broadcast_to(stamps_ref[pl.ds(block, 1), :].astype(f32), (BLOCK, BLOCK))
    query_stamps = jnp.transpose(row)
    within = lax.broadcasted_iota(jnp.int32, (BLOCK, BLOCK), 0)
    counts = (BLOCK * (listed - 1) + within + 1).astype(f32)
    return listed, query_stamps, 1.0 / counts


def causal():
    rows = lax.broadcasted_iota(jnp.int32, (BLOCK, BLOCK), 0)
    cols = lax.broadcasted_iota(jnp.int32, (BLOCK, BLOCK), 1)
    return cols <= rows


def steps_of(low, narrow):
    if not narrow:
        return list(range(1, BUCKETS))
    return [jnp.minimum(low + k, BUCKETS) for k in range(1, NARROW + 1)]


def half_bias(spread, low, narrow, bias_ref, power_ref):
    first = low if narrow else 0
    bias = jnp.full((BLOCK, BLOCK), bias_ref[first] * 0.5, f32)
    for c in steps_of(low, narrow):
        bias = jnp.where(spread >= power_ref[c], bias_ref[c] * 0.5, bias)
    return bias


def all_narrow(width_ref, slot, entries):
    widest = width_ref[slot, entries[0]]
    for entry in entries[1:]:
        widest = jnp.maximum(widest, width_ref[slot, entry])
    return widest <= NARROW


def load_pairs(parts, kv, sems):
    copies = []
    for k, part in enumerate(parts):
        rows = part.shape[0]
        copies.append(pltpu.make_async_copy(part, kv.at[pl.ds(k * rows, rows)], sems.at[k]))
    for copy in copies:
        copy.start()
    return copies


def loaded(kv, pos_ref, slot, entries):
    keys, values = [], []
    for entry in entries:
        rows = pl.ds(pl.multiple_of(pos_ref[slot, entry] * BLOCK, BLOCK), BLOCK)
        keys.append(kv[rows, 0:HEAD_DIM])
        values.append(kv[rows, HEAD_DIM : 2 * HEAD_DIM])
    return jnp.concatenate(keys, 0), jnp.concatenate(values, 0)


def members(step, count, listed, inverse):
    entries = [1 + step * count + j for j in range(count)]
    shares = [inverse * (entry < listed).astype(f32) for entry in entries]
    return [jnp.minimum(entry, LIST_MAX - 1) for entry in entries], shares


def attend_kernel(
    pos_ref, home_ref, blk_ref, low_ref, width_ref, n_ref, bias_ref, power_ref, stamps_ref, q_ref, *refs
):
    parts, (out_ref, kv, sems) = refs[:PARTS], refs[PARTS:]
    for copy in load_pairs(parts, kv, sems):
        copy.wait()
    for slot in range(2):
        listed, query_stamps, inverse = slot_setup(slot, blk_ref, n_ref, stamps_ref)
        query = q_ref[slot * BLOCK : (slot + 1) * BLOCK, :]

        def run(entries, shares, narrow):
            keys, values = loaded(kv, pos_ref, slot, entries)
            scores = nt_dot(query, keys) * (0.5 * SCALE)
            weights = []
            for j, (entry, share) in enumerate(zip(entries, shares)):
                spread = query_stamps - stamps_ref[pl.ds(blk_ref[slot, entry], 1), :].astype(f32)
                bias = half_bias(spread, low_ref[slot, entry], narrow, bias_ref, power_ref)
                half = scores[:, j * BLOCK : (j + 1) * BLOCK] + bias
                weights.append(((half + half * jnp.tanh(half)) * share).astype(bf16))
            return nn_dot(jnp.concatenate(weights, 1), values)

        def group(step, acc):
            entries, shares = members(step, FWD_GROUP, listed, inverse)
            return acc + lax.cond(
                all_narrow(width_ref, slot, entries),
                lambda: run(entries, shares, True),
                lambda: run(entries, shares, False),
            )

        total = run([0], [jnp.where(causal(), inverse, 0.0)], False)
        steps = (listed - 1 + FWD_GROUP - 1) // FWD_GROUP
        out_ref[slot * BLOCK : (slot + 1) * BLOCK, :] = lax.fori_loop(0, steps, group, total)


def grads_kernel(
    pos_ref, home_ref, blk_ref, low_ref, width_ref, n_ref, bias_ref, power_ref, stamps_ref, q_ref, g_ref, *refs
):
    kv, acc, other_ref, dq_ref, bins_ref = refs
    acc[...] = jnp.zeros(acc.shape, f32)
    bins_ref[...] = jnp.zeros(bins_ref.shape, f32)
    for slot in range(2):
        listed, query_stamps, inverse = slot_setup(slot, blk_ref, n_ref, stamps_ref)
        query = q_ref[slot * BLOCK : (slot + 1) * BLOCK, :]
        grad = g_ref[slot * BLOCK : (slot + 1) * BLOCK, :]
        query_t = jnp.transpose(query.astype(f32)).astype(bf16)
        grad_t = jnp.transpose(grad.astype(f32)).astype(bf16)

        def fold(values):
            return jnp.sum(values.reshape(BLOCK // 8, 8, BLOCK), axis=0)

        def run(entries, shares, narrow):
            keys, values = loaded(kv, pos_ref, slot, entries)
            scores = nt_dot(query, keys) * (0.5 * SCALE)
            prob_grads = nt_dot(grad, values)
            weights, grads = [], []
            for j, (entry, share) in enumerate(zip(entries, shares)):
                low = low_ref[slot, entry]
                spread = query_stamps - stamps_ref[pl.ds(blk_ref[slot, entry], 1), :].astype(f32)
                bias = half_bias(spread, low, narrow, bias_ref, power_ref)
                half = scores[:, j * BLOCK : (j + 1) * BLOCK] + bias
                th = jnp.tanh(half)
                up = 1.0 + th
                weights.append((half * up * share).astype(bf16))
                slope = up * (1.0 + half * (1.0 - th)) * (0.5 * share)
                score_grad = prob_grads[:, j * BLOCK : (j + 1) * BLOCK] * slope
                grads.append(score_grad.astype(bf16))
                above = fold(score_grad)
                before = low if narrow else 0
                for c in steps_of(low, narrow):
                    reach = fold(jnp.where(spread >= power_ref[c], score_grad, 0.0))
                    bins_ref[before] += above - reach
                    above, before = reach, c
                bins_ref[before] += above
            grads, weights = jnp.concatenate(grads, 1), jnp.concatenate(weights, 1)
            key_grads, value_grads = nn_dot(query_t, grads), nn_dot(grad_t, weights)
            for j, entry in enumerate(entries):
                at = home_ref[slot, entry]
                acc[at, 0] += key_grads[:, j * BLOCK : (j + 1) * BLOCK]
                acc[at, 1] += value_grads[:, j * BLOCK : (j + 1) * BLOCK]
            return nn_dot(grads, keys)

        def group(step, acc_q):
            entries, shares = members(step, BWD_GROUP, listed, inverse)
            return acc_q + lax.cond(
                all_narrow(width_ref, slot, entries),
                lambda: run(entries, shares, True),
                lambda: run(entries, shares, False),
            )

        total = run([0], [jnp.where(causal(), inverse, 0.0)], False)
        steps = (listed - 1 + BWD_GROUP - 1) // BWD_GROUP
        total = lax.fori_loop(0, steps, group, total)
        dq_ref[slot * BLOCK : (slot + 1) * BLOCK, :] = (total * SCALE).astype(bf16)
    half = BLOCKS // 2
    other_ref[0 : 4 * TILES] = acc[half:].reshape(4 * TILES, HEAD_DIM, BLOCK).astype(bf16)
    bins = jnp.sum(bins_ref[0:BUCKETS], axis=1)
    high = bins.astype(bf16)
    low = (bins - high.astype(f32)).astype(bf16)
    rest = jnp.zeros((BLOCK - 2 * BUCKETS, BLOCK), bf16)
    other_ref[4 * TILES] = jnp.concatenate([high, low, rest], 0)


def column(row):
    return jnp.transpose(jnp.broadcast_to(row, (BLOCK, row.shape[1])))


def norm_kernel(
    sums_ref, attended_ref, gated_grad_ref, gate_ref, cot_ref, gated_ref, grad_u_ref, grad_ref, w_ref
):
    sums = jnp.sum(sums_ref[...], axis=0) * (1.0 / D)
    mean, power, first, product = [column(sums[k : k + 1, :]) for k in range(4)]
    inverse = lax.rsqrt(power - mean * mean + EPS)
    second = inverse * (product - mean * first)
    gate = gate_ref[...].astype(f32)
    gated_grad = gated_grad_ref[...]
    normed = (attended_ref[...] - mean) * inverse
    gated = normed * gate
    gated_ref[...] = gated.astype(bf16)
    grad_u_ref[...] = (gated_grad * normed).astype(bf16)
    grad_ref[...] = ((gated_grad * gate - first - normed * second) * inverse).astype(bf16)
    gated_t = jnp.transpose(gated).astype(bf16)
    for k in range(8):
        w_ref[k] = nn_dot(gated_t, cot_ref[:, k * BLOCK : (k + 1) * BLOCK]).astype(bf16)


def chip_kernel(own_ref, other_ref, weight_ref, bins_ref, out_ref):
    split = TILES * HEAD_DIM
    weight = jnp.sum(weight_ref[...].astype(f32), axis=0).astype(bf16)
    tail = other_ref[4 * TILES].astype(f32)
    bins = jnp.sum(bins_ref[0:BUCKETS], axis=1)
    bins = bins + tail[0:BUCKETS] + tail[BUCKETS : 2 * BUCKETS]
    high = bins.astype(bf16)
    low = (bins - high.astype(f32)).astype(bf16)
    for k in range(4):
        for j in range(TILES):
            tile = own_ref[(k * TILES + j) // 2, j % 2] + other_ref[k * TILES + j].astype(f32)
            out_ref[k, j * HEAD_DIM : (j + 1) * HEAD_DIM] = tile.astype(bf16)
        out_ref[k, split : split + HEAD_DIM] = weight
        out_ref[k, split + HEAD_DIM : split + HEAD_DIM + BUCKETS] = high
        out_ref[k, split + HEAD_DIM + BUCKETS : split + HEAD_DIM + 2 * BUCKETS] = low


def project_kernel(back_ref, weight_ref, out_ref):
    gated = jnp.concatenate([back_ref[h, :, 4 * HEAD_DIM :] for h in range(HEADS)], 1)
    for k in range(8):
        rows = [weight_ref[k, d, h] for h in range(HEADS) for d in range(4)]
        product = nn_dot(gated, jnp.concatenate(rows, 0))
        out_ref[:, k * BLOCK : (k + 1) * BLOCK] = product.astype(bf16)


SMEM = functools.partial(pl.BlockSpec, memory_space=pltpu.SMEM)
VMEM = functools.partial(pl.BlockSpec, memory_space=pltpu.VMEM)
ANY = functools.partial(pl.BlockSpec, memory_space=pl.ANY)


def attend(tables, query, parts):
    return pl.pallas_call(
        attend_kernel,
        out_shape=(
            jax.ShapeDtypeStruct((2 * BLOCK, HEAD_DIM), f32),
            jax.ShapeDtypeStruct((BLOCKS * BLOCK, 2 * HEAD_DIM), bf16),
        ),
        in_specs=[SMEM()] * 8 + [VMEM()] * 2 + [ANY()] * PARTS,
        out_specs=(VMEM(), VMEM()),
        scratch_shapes=[
            pltpu.SemaphoreType.DMA((PARTS,)),
        ],
        compiler_params=pltpu.CompilerParams(vmem_limit_bytes=12 * MIB),
        cost_estimate=pl.CostEstimate(
            flops=5 * 10**9, bytes_accessed=3 << 20, transcendentals=48 * BLOCK**2
        ),
        name="attend",
    )(*tables, query, *parts)


def attend_grads(tables, query, grad, pairs):
    return pl.pallas_call(
        grads_kernel,
        out_shape=(
            jax.ShapeDtypeStruct((BLOCKS, 2, HEAD_DIM, BLOCK), f32),
            jax.ShapeDtypeStruct((4 * TILES + 1, HEAD_DIM, BLOCK), bf16),
            jax.ShapeDtypeStruct((2 * BLOCK, HEAD_DIM), bf16),
            jax.ShapeDtypeStruct((BUCKETS + 1, 8, BLOCK), f32),
        ),
        in_specs=[SMEM()] * 8 + [VMEM()] * 4,
        out_specs=(VMEM(),) * 4,
        compiler_params=pltpu.CompilerParams(vmem_limit_bytes=24 * MIB),
        cost_estimate=pl.CostEstimate(
            flops=12 * 10**9, bytes_accessed=6 << 20, transcendentals=48 * BLOCK**2
        ),
        name="attend_grads",
    )(*tables, query, grad, pairs)


def whole_call(kernel, out_shape, name, *args):
    return pl.pallas_call(
        kernel,
        out_shape=out_shape,
        in_specs=[VMEM()] * len(args),
        out_specs=jax.tree.map(lambda _: VMEM(), out_shape),
        compiler_params=pltpu.CompilerParams(vmem_limit_bytes=12 * MIB),
        cost_estimate=pl.CostEstimate(flops=10**9, bytes_accessed=4 * MIB, transcendentals=0),
        name=name,
    )(*args)


def exchange(values, axes):
    return lax.all_to_all(values, axes, split_axis=0, concat_axis=0, tiled=True)


def to_all(values, axes, count):
    return exchange(jnp.broadcast_to(values[None], (count,) + values.shape), axes)


def swap_core(values):
    return lax.ppermute(values, "core", [(0, 1), (1, 0)])


def shift_x(values, by):
    return lax.ppermute(values, "x", [(i, (i + by) % 4) for i in range(4)])


def flip(values, axis, by):
    return lax.ppermute(values, axis, [(i, i ^ by) for i in range(lax.axis_size(axis))])


def after(values, *others):
    return lax.optimization_barrier((values,) + others)[0]


def joined(values, theirs, axis, by):
    late = (lax.axis_index(axis) & by) != 0
    return jnp.concatenate([jnp.where(late, theirs, values), jnp.where(late, values, theirs)], 1)


def halves(bias):
    high = lax.reduce_precision(bias, exponent_bits=8, mantissa_bits=7)
    return jnp.concatenate([high, bias - high], 0)


def whole(rows):
    return rows[:BUCKETS] + rows[BUCKETS:]


def tables_of(lists, blk, pos, home, run, stamp_blocks, time_bias):
    listed = jnp.sum((lists >= 0).astype(jnp.int32), 1)
    powers = 2 ** jnp.arange(BUCKETS - 1, dtype=jnp.int32)
    own = lax.dynamic_slice_in_dim(stamp_blocks, run * 2, 2, 0)
    first = stamp_blocks[:, 0][blk]
    last = stamp_blocks[:, BLOCK - 1][blk]
    least = jnp.maximum(own[:, :1] - last, 0)
    most = own[:, BLOCK - 1 :] - first
    low = jnp.sum((least[:, :, None] >= powers).astype(jnp.int32), -1)
    high = jnp.sum((most[:, :, None] >= powers).astype(jnp.int32), -1)
    bias = jnp.concatenate([time_bias, jnp.zeros((1,), f32)])
    limits = jnp.concatenate([jnp.zeros((1,), jnp.int32), powers, jnp.full((1,), 1 << 30)])
    return (pos, home, blk, low, high - low, listed, bias, limits.astype(f32), stamp_blocks)


def body(projected, cotangent, out_weight, time_bias, block_lists, stamps):
    tokens = projected.shape[1]
    x, zh, core = lax.axis_index("x"), lax.axis_index("zh"), lax.axis_index("core")
    run = (x * 2 + zh) * 2 + core

    by_head = projected[0].reshape(tokens, 4, HEADS, HEAD_DIM).transpose(2, 0, 1, 3)
    pairs = by_head[:, :, 1:3].reshape(HEADS, tokens, 2 * HEAD_DIM)
    pairs = exchange(jnp.concatenate([pairs, pairs], 0), ZLINE).reshape(4 * BLOCK, 2 * HEAD_DIM)
    dp = lax.axis_index("dp")
    slab = lax.dynamic_slice(out_weight, (dp * tokens, (x * 2 + core) * BLOCK), (tokens, BLOCK))
    rest = jnp.concatenate([cotangent[0], slab], 1)
    rest = jnp.broadcast_to(rest, (HEADS,) + rest.shape)
    rest = exchange(jnp.concatenate([by_head[:, :, 0], by_head[:, :, 3], rest], 2), "head")
    slabs = rest[:, :, 2 * HEAD_DIM + D :].reshape(HEADS * tokens, BLOCK)
    all_weight = lax.all_gather(slabs, ("x", "core", "dp"), axis=0, tiled=True)
    all_weight = all_weight.reshape(8, 4, HEADS, tokens, BLOCK)
    query = rest[:, :, :HEAD_DIM].reshape(2 * BLOCK, HEAD_DIM)
    gate = rest[:, :, HEAD_DIM : 2 * HEAD_DIM].reshape(2 * BLOCK, HEAD_DIM)
    cot = rest[:, :, 2 * HEAD_DIM : 2 * HEAD_DIM + D].reshape(2 * BLOCK, D)
    own_pairs = jnp.concatenate([pairs] + [shift_x(pairs, by) for by in SHIFTS], 0)
    parts = [own_pairs, swap_core(own_pairs)]

    lists = lax.dynamic_slice_in_dim(block_lists[0], run * 2, 2, 0)
    blk = jnp.maximum(lists, 0)
    side = ((blk // 2) % 2) ^ core
    ahead = (x - blk // 8) & 3
    place = jnp.where(ahead == 2, 3, jnp.where(ahead == 3, 2, ahead))
    pos = ((side * 4 + place) * 2 + (blk // 4) % 2) * 2 + blk % 2
    home = ((side * 4 + blk // 8) * 2 + (blk // 4) % 2) * 2 + blk % 2
    stamp_blocks = stamps[0].reshape(BLOCKS, BLOCK)
    tables = tables_of(lists, blk, pos, home, run, stamp_blocks, time_bias[0])

    attended, pairs = attend(tables, query, parts)

    gated_grad = nt_dot(cot, out_weight)
    normed_grad = gated_grad * gate.astype(f32)
    sums = jnp.stack(
        [
            jnp.sum(attended, 1),
            jnp.sum(attended * attended, 1),
            jnp.sum(normed_grad, 1),
            jnp.sum(normed_grad * attended, 1),
        ]
    )
    sums = to_all(sums, "head", HEADS).reshape(HEADS, 4, 2 * BLOCK)
    rows = jax.ShapeDtypeStruct((2 * BLOCK, HEAD_DIM), bf16)
    tiles = jax.ShapeDtypeStruct((8, HEAD_DIM, BLOCK), bf16)
    gated, grad_u, attended_grad, weight_part = whole_call(
        norm_kernel, (rows, rows, rows, tiles), "norm", sums, attended, gated_grad, gate, cot
    )
    weight_part = exchange(weight_part, ("core", "dp"))

    own_grads, other_grads, grad_q, bins = attend_grads(tables, query, attended_grad, pairs)
    theirs = swap_core(other_grads)
    split = TILES * HEAD_DIM
    chip = jax.ShapeDtypeStruct((4, split + HEAD_DIM + 2 * BUCKETS, BLOCK), bf16)
    chip = whole_call(chip_kernel, chip, "chip", own_grads, theirs, weight_part, bins)
    line = jnp.sum(exchange(chip, "x").reshape(chip.shape).astype(f32), 0)

    pair = line[:split].reshape(2, split // 2, BLOCK)
    own_tiles = lax.dynamic_index_in_dim(pair, zh, 0, False)
    sent = lax.dynamic_index_in_dim(pair, 1 - zh, 0, False)
    weight_part, bias_part = line[split : split + HEAD_DIM], whole(line[split + HEAD_DIM :])
    sent = jnp.concatenate([sent, weight_part, halves(bias_part)], 0).astype(bf16)
    theirs = flip(sent, "zh", 1).astype(f32)
    own_tiles = own_tiles + theirs[: split // 2]
    theirs = theirs[split // 2 :]
    columns = weight_part.astype(bf16).astype(f32) + theirs[:HEAD_DIM]
    bias_part = jnp.sum(bias_part + whole(theirs[HEAD_DIM:]), 1)

    for by in (1, 2):
        sent = jnp.pad(bias_part[None], ((0, 7), (0, columns.shape[1] - BUCKETS)))
        theirs = flip(jnp.concatenate([columns, sent], 0), "dp", by)
        bias_part = bias_part + theirs[HEAD_DIM, :BUCKETS]
        columns = joined(columns, theirs[:HEAD_DIM], "dp", by)
    bias_grad = bias_part[None]
    weight_grad = joined(columns, swap_core(columns), "core", 1)

    line = own_tiles.astype(bf16).reshape(2, 2, HEAD_DIM, BLOCK)
    line = line.transpose(0, 3, 1, 2).reshape(HEADS, tokens, 2 * HEAD_DIM)
    rows = jnp.concatenate([grad_q, grad_u, gated], 1).reshape(HEADS, tokens, 3 * HEAD_DIM)
    back = exchange(jnp.concatenate([line, rows], 2), "head")
    rows = back[:, :, 2 * HEAD_DIM :]
    pair_grads = back[:, :, : 2 * HEAD_DIM].astype(f32)
    grad_k = (pair_grads[:, :, :HEAD_DIM] * SCALE).astype(bf16)
    grad_v = pair_grads[:, :, HEAD_DIM:].astype(bf16)
    grad_u = rows[:, :, HEAD_DIM : 2 * HEAD_DIM]
    grads = jnp.stack([rows[:, :, :HEAD_DIM], grad_k, grad_v, grad_u], 0)
    input_grads = grads.transpose(2, 0, 1, 3).reshape(1, tokens, 4, D)
    layer_out = jax.ShapeDtypeStruct((tokens, D), bf16)
    layer_out = whole_call(project_kernel, layer_out, "project", back, all_weight)
    layer_out = layer_out.reshape(1, tokens, D)
    return (layer_out, input_grads, weight_grad, bias_grad)


def solution(mesh):
    fine = Mesh(
        mesh.devices.reshape(4, 4, 2, 2, 8), ("dp", "x", "zh", "core", "head")
    )
    run = SEQ + ("head",)
    in_specs = (
        P("dp", run, None, None),
        P("dp", run, None),
        P("head", None),
        P("head", None),
        P("dp", None, None),
        P("dp", None),
    )
    out_specs = (
        P("dp", run, None),
        P("dp", run, None, None),
        P("head", None),
        P("head", None),
    )
    return jax.shard_map(body, mesh=fine, in_specs=in_specs, out_specs=out_specs, check_vma=False)
```
